512 devices in a mesh: qrow: 8 (over x, y_lo), kcol: 64 (over z, y_hi, core).
Axes of the slice: x: 4, y: 4 (y_hi: 2, y_lo: 2; y = y_hi * 2 + y_lo), z: 16, core: 2. Of those that a mesh axis runs over, the one named last changes fastest.
Arguments:
- queries: bfloat16 [32768, 256], P(('qrow', 'kcol')), may hold values from -6 to 6
- keys: bfloat16 [32768, 128], P(('kcol', 'qrow')), may hold values from -6 to 6
- values: bfloat16 [32768, 128], P(('kcol', 'qrow')), may hold values from -6 to 6
- out_grad: bfloat16 [32768, 256], P(('qrow', 'kcol')), may hold values from -6 to 6
- log_sum: float32 [32768, 2], P(('qrow', 'kcol')), may hold values from 4.5 to 6.5
- delta: float32 [32768, 2], P(('qrow', 'kcol')), may hold values from -24 to 24
- block_table: int32 [1024], replicated, may hold values from 0 to 1023, as said below
Outputs:
- q_grad: bfloat16 [32768, 256], P(('qrow', 'kcol'))
- k_grad: bfloat16 [32768, 128], P(('kcol', 'qrow'))
- v_grad: bfloat16 [32768, 128], P(('kcol', 'qrow'))
The draws below stay inside these ranges and needn't reach their ends.
Inputs may be any that keep to these rules, and one draw needn't show every extreme that they name: `block_table`: a permutation of 0 to 1023 in which entries 2 d and 2 d + 1 sum to 1023 for every d.
All inputs are finite; a program needn't handle non-finite values.
Results may differ from the reference program's by a relative error of at most 0.0049.
Values may be sent and summed in bfloat16 or wider, within the bound.
No kernel may reach another device: no remote copies, remote signals or barrier semaphores. Data moves between devices by JAX's collectives and lax.ppermute only.
A program may use at most 64 MiB of HBM per device.

```python
import math
import jax
import jax.numpy as jnp
from jax import lax

HEADS = 2
HD = 128
ROWS_DEV = 64
SEQ = 32768
NBLK = 1024


def draw_block_table(key, part):
    key = jax.random.fold_in(key, 11)
    order = jax.random.permutation(key, NBLK // 2).astype(jnp.int32)
    partner = (NBLK - 1 - order).astype(jnp.int32)
    return jnp.stack([order, partner], axis=1).reshape(NBLK)


def block_levels(rng, extent, cuts, smallest, high):
    level = 1.0
    for dim, parts in cuts:
        heights = jax.random.uniform(jax.random.fold_in(jax.random.fold_in(rng, 6), dim), (parts,), jnp.float32, smallest / len(cuts), high / len(cuts))
        level = level * jnp.repeat(jnp.exp(heights), extent[dim] // parts).reshape((-1,) + (1,) * (len(extent) - 1 - dim))
    return level


def normal_values(key, dims, width, reach, cuts=(), kind=jnp.bfloat16):
    result = width * jax.random.normal(key, dims, jnp.float32)
    if cuts:
        result = result * block_levels(key, dims, cuts, -0.22, 0.18)
    return jnp.clip(result, -reach, reach).astype(kind)


def setup_inputs(seed: int = 0) -> dict:
    seeds = jax.random.split(jax.random.key(seed), 8)
    queries = normal_values(seeds[0], (SEQ, HEADS * HD), 1.0, 6.0, ((0, 512),))
    keys = normal_values(seeds[1], (SEQ, HD), 1.0, 6.0, ((0, 512),))
    values = normal_values(seeds[2], (SEQ, HD), 1.0, 6.0, ((0, 512),))
    out_grad = normal_values(seeds[3], (SEQ, HEADS * HD), 1.0, 6.0, ((0, 512),))
    log_sum = jnp.clip(4.5 + 2.0 * jax.random.uniform(seeds[4], (SEQ, HEADS), jnp.float32) ** block_levels(seeds[4], (SEQ, HEADS), ((0, 512),), -0.2, 0.2), 4.5, 6.5)
    delta = normal_values(seeds[5], (SEQ, HEADS), 4.0, 24.0, ((0, 512),), jnp.float32)
    block_table = draw_block_table(jax.random.fold_in(seeds[7], 71), 0)
    return {"queries": queries, "keys": keys, "values": values, "out_grad": out_grad, "log_sum": log_sum, "delta": delta, "block_table": block_table}


def reference(queries, keys, values, out_grad, log_sum, delta, block_table):
    total = queries.shape[0]
    half = ROWS_DEV // 2
    rows_index = jnp.arange(total, dtype=jnp.int32)
    position = block_table[rows_index // half].astype(jnp.int32) * half + rows_index % half
    scale = HD ** -0.5
    key_full = keys.astype(jnp.float32)
    value_full = values.astype(jnp.float32)
    step = math.gcd(total, 256)
    count = total // step
    query_blocks = queries.reshape(count, step, HEADS, HD)
    grad_blocks = out_grad.reshape(count, step, HEADS, HD)
    lse_blocks = log_sum.reshape(count, step, HEADS)
    delta_blocks = delta.reshape(count, step, HEADS)
    pos_blocks = position.reshape(count, step)

    def one_block(carry, pieces):
        key_acc, value_acc = carry
        query_part, grad_part, lse_part, delta_part, pos_part = pieces
        query_float = query_part.astype(jnp.float32)
        grad_float = grad_part.astype(jnp.float32)
        scores = jnp.einsum("qhd,kd->hqk", query_float, key_full) * scale
        live = position[None, :] <= pos_part[:, None]
        probs = jnp.where(live[None], jnp.exp(scores - lse_part.T[:, :, None]), jnp.float32(0.0))
        probs_b = probs.astype(jnp.bfloat16).astype(jnp.float32)
        value_acc = value_acc + jnp.einsum("hqk,qhd->kd", probs_b, grad_float)
        dprobs = jnp.einsum("qhd,kd->hqk", grad_float, value_full)
        dscores = (probs * (dprobs - delta_part.T[:, :, None])).astype(jnp.bfloat16).astype(jnp.float32)
        query_grad = jnp.einsum("hqk,kd->qhd", dscores, key_full)
        key_acc = key_acc + jnp.einsum("hqk,qhd->kd", dscores, query_float)
        return (key_acc, value_acc), query_grad

    start = (jnp.zeros((total, HD), jnp.float32), jnp.zeros((total, HD), jnp.float32))
    (key_acc, value_acc), query_grads = lax.scan(
        one_block, start, (query_blocks, grad_blocks, lse_blocks, delta_blocks, pos_blocks))
    q_grad = (query_grads.reshape(total, HEADS * HD) * scale).astype(jnp.bfloat16)
    k_grad = (key_acc * scale).astype(jnp.bfloat16)
    v_grad = value_acc.astype(jnp.bfloat16)
    return q_grad, k_grad, v_grad
```

```python
import jax
import jax.numpy as jnp
from jax import lax
from jax.experimental import pallas as pl
from jax.experimental.pallas import tpu as pltpu
from jax.sharding import Mesh, PartitionSpec as P

HEADS = 2
HD = 128
HALF = 32
SCALE = HD ** (-0.5)
LOG2E = 1.4426950408889634
PIECES = 3
QT = 256
KT = 256
PLANE = ("x", "yl", "yh")


def dot(a, b):
    return jnp.dot(a, b, preferred_element_type=jnp.float32)


def dot_nt(a, b):
    return lax.dot_general(a, b, (((1,), (1,)), ((), ())), preferred_element_type=jnp.float32)


def tile_kernel(first, last, meta, q_ref, kv_ref, posq_ref, posk_ref, *rest):
    rest = list(rest)
    if not first:
        dkv_in = rest.pop(0)
    dq_ref, dkv_ref, qs, gs, st, lse, dlt, ks, vs, kt, dqt, dk, dv = rest
    rows_q = q_ref.shape[0]
    rows_k = kv_ref.shape[0]
    nbq = rows_q // HALF
    nbk = rows_k // HALF

    def sort_q(s, c):
        src = pl.multiple_of(meta[0, s] * HALF, HALF)
        dst = pl.multiple_of(s * HALF, HALF)
        for h in range(HEADS):
            qs[h, pl.ds(dst, HALF), :] = q_ref[pl.ds(src, HALF), h * HD:(h + 1) * HD]
            gs[h, pl.ds(dst, HALF), :] = q_ref[pl.ds(src, HALF), (HEADS + h) * HD:(HEADS + h + 1) * HD]
        st[pl.ds(dst, HALF), :] = q_ref[pl.ds(src, HALF), 2 * HEADS * HD:]
        return c

    lax.fori_loop(0, nbq, sort_q, 0, unroll=4)

    def sort_k(s, c):
        src = pl.multiple_of(meta[2, s] * HALF, HALF)
        dst = pl.multiple_of(s * HALF, HALF)
        ks[pl.ds(dst, HALF), :] = kv_ref[pl.ds(src, HALF), :HD]
        vs[pl.ds(dst, HALF), :] = kv_ref[pl.ds(src, HALF), HD:]
        return c

    lax.fori_loop(0, nbk, sort_k, 0, unroll=4)

    for t in range(rows_q // 128):
        cut = slice(t * 128, (t + 1) * 128)
        turned = st[cut, :].astype(jnp.float32).T
        for h in range(HEADS):
            a = h * PIECES
            b = (HEADS + h) * PIECES
            lse[h:h + 1, cut] = (turned[a:a + 1] + turned[a + 1:a + 2] + turned[a + 2:a + 3]) * LOG2E
            dlt[h:h + 1, cut] = turned[b:b + 1] + turned[b + 1:b + 2] + turned[b + 2:b + 3]
    for t in range(rows_k // 128):
        cut = slice(t * 128, (t + 1) * 128)
        kt[:, cut] = ks[cut, :].astype(jnp.float32).T.astype(jnp.bfloat16)

    if first:
        dk[...] = jnp.zeros_like(dk)
        dv[...] = jnp.zeros_like(dv)
    else:
        dk[...] = dkv_in[:, :HD]
        dv[...] = dkv_in[:, HD:]
    dqt[...] = jnp.zeros_like(dqt)

    kb = KT // HALF
    qb = QT // HALF

    def over_q(j, c):
        q0 = pl.multiple_of(j * QT, QT)
        top = meta[1, j * qb + qb - 1]
        live = jnp.int32(0)
        for i in range(rows_k // KT):
            live += (meta[3, i * kb] <= top).astype(jnp.int32)
        posq = posq_ref[:, pl.ds(q0, QT)]

        def over_k(i, c):
            k0 = pl.multiple_of(i * KT, KT)
            k = ks[pl.ds(k0, KT), :]
            v = vs[pl.ds(k0, KT), :]
            mask = posk_ref[pl.ds(k0, KT), :] <= posq
            dv_t = dv[pl.ds(k0, KT), :]
            dk_t = dk[pl.ds(k0, KT), :]
            for h in range(HEADS):
                q = qs[h, pl.ds(q0, QT), :]
                g = gs[h, pl.ds(q0, QT), :]
                s = dot_nt(k, q)
                p = jnp.where(mask, jnp.exp2(s * (SCALE * LOG2E) - lse[h:h + 1, pl.ds(q0, QT)]), 0.0)
                dv_t = dv_t + dot(p.astype(jnp.bfloat16), g)
                dp = dot_nt(v, g)
                ds = (p * (dp - dlt[h:h + 1, pl.ds(q0, QT)])).astype(jnp.bfloat16)
                dk_t = dk_t + dot(ds, q)
                dqt[h, :, pl.ds(q0, QT)] += dot(kt[:, pl.ds(k0, KT)], ds)
            dv[pl.ds(k0, KT), :] = dv_t
            dk[pl.ds(k0, KT), :] = dk_t
            return c

        lax.fori_loop(0, live, over_k, 0)
        for h in range(HEADS):
            back = dqt[h, :, pl.ds(q0, QT)].T.astype(jnp.bfloat16)
            for b in range(qb):
                dst = pl.multiple_of(meta[0, j * qb + b] * HALF, HALF)
                dq_ref[pl.ds(dst, HALF), h * HD:(h + 1) * HD] = back[b * HALF:(b + 1) * HALF]
        return c

    lax.fori_loop(0, rows_q // QT, over_q, 0)

    if last:
        def spread_k(s, c):
            dst = pl.multiple_of(meta[2, s] * HALF, HALF)
            src = pl.multiple_of(s * HALF, HALF)
            dkv_ref[pl.ds(dst, HALF), :HD] = dk[pl.ds(src, HALF), :].astype(jnp.bfloat16)
            dkv_ref[pl.ds(dst, HALF), HD:] = dv[pl.ds(src, HALF), :].astype(jnp.bfloat16)
            return c

        lax.fori_loop(0, nbk, spread_k, 0, unroll=4)
    else:
        dkv_ref[:, :HD] = dk[...]
        dkv_ref[:, HD:] = dv[...]


def tile_grads(first, last, meta, qg, kv, posq, posk, dkv_in=None):
    rows_q = qg.shape[0]
    rows_k = kv.shape[0]
    vmem = pl.BlockSpec(memory_space=pltpu.VMEM)
    args = [meta, qg, kv, posq, posk] + ([] if first else [dkv_in])
    bf, f32 = jnp.bfloat16, jnp.float32

    def body(*refs):
        tile_kernel(first, last, *refs)

    return pl.pallas_call(
        body,
        out_shape=(
            jax.ShapeDtypeStruct((rows_q, HEADS * HD), bf),
            jax.ShapeDtypeStruct((rows_k, 2 * HD), bf if last else f32),
        ),
        in_specs=[pl.BlockSpec(memory_space=pltpu.SMEM)] + [vmem] * (len(args) - 1),
        out_specs=(vmem, vmem),
        scratch_shapes=[
            pltpu.VMEM((HEADS, rows_q, HD), bf),
            pltpu.VMEM((HEADS, rows_q, HD), bf),
            pltpu.VMEM((rows_q, 128), bf),
            pltpu.VMEM((8, rows_q), f32),
            pltpu.VMEM((8, rows_q), f32),
            pltpu.VMEM((rows_k, HD), bf),
            pltpu.VMEM((rows_k, HD), bf),
            pltpu.VMEM((HD, rows_k), bf),
            pltpu.VMEM((HEADS, HD, rows_q), f32),
            pltpu.VMEM((rows_k, HD), f32),
            pltpu.VMEM((rows_k, HD), f32),
        ],
        compiler_params=pltpu.CompilerParams(vmem_limit_bytes=40 * 1024 * 1024),
        cost_estimate=pl.CostEstimate(
            flops=rows_q * HEADS * rows_k * HD * 5,
            bytes_accessed=4 * 1024 * 1024,
            transcendentals=rows_q * HEADS * rows_k // 2,
        ),
    )(*args)


def in_order(entries):
    n = entries.shape[0]
    rank = jnp.sum((entries[None, :] < entries[:, None]).astype(jnp.int32), axis=1)
    hit = rank[None, :] == jnp.arange(n, dtype=jnp.int32)[:, None]
    place = jnp.arange(n, dtype=jnp.int32)
    order = jnp.sum(jnp.where(hit, place[None, :], 0), axis=1)
    ordered = jnp.sum(jnp.where(hit, entries[None, :], 0), axis=1)
    return order, ordered


def positions(ordered):
    return (ordered[:, None] * HALF + jnp.arange(HALF, dtype=jnp.int32)[None, :]).reshape(-1)


def pieces(x):
    out = []
    for _ in range(PIECES):
        part = lax.reduce_precision(x, 8, 7)
        out.append(part.astype(jnp.bfloat16))
        x = x - part
    return out


def exchange(x, axes):
    return lax.all_to_all(x, axes, split_axis=0, concat_axis=0, tiled=True)


def to_all(x, axes, n):
    return exchange(jnp.broadcast_to(x[None], (n,) + x.shape), axes).reshape(n * x.shape[0], x.shape[1])


def local(queries, keys, values, out_grad, log_sum, delta, block_table):
    rows = queries.shape[0]
    nx, nyl, nz, nyh, nc = (lax.axis_size(a) for a in ("x", "yl", "z", "yh", "core"))
    ixy = lax.axis_index(("x", "yl"))
    iz, iyh, ic = (lax.axis_index(a) for a in ("z", "yh", "core"))
    plane = nx * nyl * nyh

    stats = []
    split = [pieces(log_sum), pieces(delta)]
    for parts in split:
        for h in range(HEADS):
            for k in range(PIECES):
                stats.append(parts[k][:, h:h + 1])
    stats.append(jnp.zeros((rows, 128 - 2 * HEADS * PIECES), jnp.bfloat16))
    packed = jnp.concatenate([queries, out_grad] + stats, axis=1)
    q_own = to_all(packed, PLANE, plane)
    kv = to_all(jnp.concatenate([keys, values], axis=1), "z", nz)
    q_sib = lax.ppermute(q_own, "core", [(0, 1), (1, 0)])

    q_table = block_table.reshape(nx * nyl, nz, nyh, nc, 2)
    q_table = lax.dynamic_index_in_dim(q_table, iz, 1, keepdims=False)
    k_table = block_table.reshape(nz, nyh, nc, nx * nyl, 2)
    k_table = lax.dynamic_index_in_dim(k_table, iyh, 1, keepdims=False)
    k_table = lax.dynamic_index_in_dim(k_table, ic, 1, keepdims=False)
    k_table = lax.dynamic_index_in_dim(k_table, ixy, 1, keepdims=False).reshape(-1)
    order_k, sorted_k = in_order(k_table)
    posk = positions(sorted_k)[:, None]
    metas, posqs = [], []
    for c in (ic, nc - 1 - ic):
        table = lax.dynamic_index_in_dim(q_table, c, 2, keepdims=False).reshape(-1)
        order_q, sorted_q = in_order(table)
        metas.append(jnp.stack([order_q, sorted_q, order_k, sorted_k]))
        posqs.append(positions(sorted_q)[None, :])

    dq_own, dkv = tile_grads(True, False, metas[0], q_own, kv, posqs[0], posk)
    dq_sib, dkv = tile_grads(False, True, metas[1], q_sib, kv, posqs[1], posk, dkv)

    first = jnp.where(ic == 0, dq_own, dq_sib)
    second = jnp.where(ic == 0, dq_sib, dq_own)
    dq_all = jnp.concatenate([first, second], axis=0).reshape(nc * plane, rows, HEADS * HD)
    dq_in = exchange(dq_all, ("core",) + PLANE)
    dkv_in = exchange(dkv.reshape(nz, rows, 2 * HD), "z")
    q_grad = (jnp.sum(dq_in.astype(jnp.float32), axis=0) * SCALE).astype(jnp.bfloat16)
    dkv_sum = jnp.sum(dkv_in.astype(jnp.float32), axis=0)
    k_grad = (dkv_sum[:, :HD] * SCALE).astype(jnp.bfloat16)
    v_grad = dkv_sum[:, HD:].astype(jnp.bfloat16)
    return (q_grad, k_grad, v_grad)


def solution(mesh):
    fine = Mesh(mesh.devices.reshape(4, 2, 16, 2, 2), ("x", "yl", "z", "yh", "core"))
    q_rows = P(("x", "yl", "z", "yh", "core"), None)
    k_rows = P(("z", "yh", "core", "x", "yl"), None)
    return jax.shard_map(
        local,
        mesh=fine,
        in_specs=(q_rows, k_rows, k_rows, q_rows, q_rows, q_rows, P()),
        out_specs=(q_rows, k_rows, k_rows),
        check_vma=False,
    )
```

```python
import jax
import jax.numpy as jnp
from jax import lax
from jax.experimental import pallas as pl
from jax.experimental.pallas import tpu as pltpu
from jax.sharding import Mesh, PartitionSpec as P

HEADS = 2
HD = 128
HALF = 32
SCALE = HD ** (-0.5)
LOG2E = 1.4426950408889634
PIECES = 3
QT = 256
KT = 256


def dot(a, b):
    return jnp.dot(a, b, preferred_element_type=jnp.float32)


def dot_nt(a, b):
    return lax.dot_general(a, b, (((1,), (1,)), ((), ())), preferred_element_type=jnp.float32)


def tile_kernel(first, last, meta, q_ref, kv_ref, posq_ref, posk_ref, *rest):
    rest = list(rest)
    if not first:
        dkv_in = rest.pop(0)
    dq_ref, dkv_ref, qs, gs, st, lse, dlt, ks, vs, kt, dqt, dk, dv = rest
    rows_q = q_ref.shape[0]
    rows_k = kv_ref.shape[0]
    nbq = rows_q // HALF
    nbk = rows_k // HALF

    def sort_q(s, c):
        src = pl.multiple_of(meta[0, s] * HALF, HALF)
        dst = pl.multiple_of(s * HALF, HALF)
        for h in range(HEADS):
            qs[h, pl.ds(dst, HALF), :] = q_ref[pl.ds(src, HALF), h * HD:(h + 1) * HD]
            gs[h, pl.ds(dst, HALF), :] = q_ref[pl.ds(src, HALF), (HEADS + h) * HD:(HEADS + h + 1) * HD]
        st[pl.ds(dst, HALF), :] = q_ref[pl.ds(src, HALF), 2 * HEADS * HD:]
        return c

    lax.fori_loop(0, nbq, sort_q, 0, unroll=4)

    def sort_k(s, c):
        src = pl.multiple_of(meta[2, s] * HALF, HALF)
        dst = pl.multiple_of(s * HALF, HALF)
        ks[pl.ds(dst, HALF), :] = kv_ref[pl.ds(src, HALF), :HD]
        vs[pl.ds(dst, HALF), :] = kv_ref[pl.ds(src, HALF), HD:]
        return c

    lax.fori_loop(0, nbk, sort_k, 0, unroll=4)

    for t in range(rows_q // 128):
        cut = slice(t * 128, (t + 1) * 128)
        turned = st[cut, :].astype(jnp.float32).T
        for h in range(HEADS):
            a, b, n = h, HEADS + h, 2 * HEADS
            lse[h:h + 1, cut] = (turned[a:a + 1] + turned[a + n:a + n + 1] + turned[a + 2 * n:a + 2 * n + 1]) * LOG2E
            dlt[h:h + 1, cut] = turned[b:b + 1] + turned[b + n:b + n + 1] + turned[b + 2 * n:b + 2 * n + 1]
    for t in range(rows_k // 128):
        cut = slice(t * 128, (t + 1) * 128)
        kt[:, cut] = ks[cut, :].astype(jnp.float32).T.astype(jnp.bfloat16)

    if first:
        dk[...] = jnp.zeros_like(dk)
        dv[...] = jnp.zeros_like(dv)
    else:
        dk[...] = dkv_in[:, :HD]
        dv[...] = dkv_in[:, HD:]
    dqt[...] = jnp.zeros_like(dqt)

    kb = KT // HALF
    qb = QT // HALF

    def over_q(j, c):
        q0 = pl.multiple_of(j * QT, QT)
        top = meta[1, j * qb + qb - 1]
        live = jnp.int32(0)
        for i in range(rows_k // KT):
            live += (meta[3, i * kb] <= top).astype(jnp.int32)
        posq = posq_ref[:, pl.ds(q0, QT)]

        def over_k(i, c):
            k0 = pl.multiple_of(i * KT, KT)
            k = ks[pl.ds(k0, KT), :]
            v = vs[pl.ds(k0, KT), :]
            mask = posk_ref[pl.ds(k0, KT), :] <= posq
            dv_t = dv[pl.ds(k0, KT), :]
            dk_t = dk[pl.ds(k0, KT), :]
            for h in range(HEADS):
                q = qs[h, pl.ds(q0, QT), :]
                g = gs[h, pl.ds(q0, QT), :]
                s = dot_nt(k, q)
                p = jnp.where(mask, jnp.exp2(s * (SCALE * LOG2E) - lse[h:h + 1, pl.ds(q0, QT)]), 0.0)
                dv_t = dv_t + dot(p.astype(jnp.bfloat16), g)
                dp = dot_nt(v, g)
                ds = (p * (dp - dlt[h:h + 1, pl.ds(q0, QT)])).astype(jnp.bfloat16)
                dk_t = dk_t + dot(ds, q)
                dqt[h, :, pl.ds(q0, QT)] += dot(kt[:, pl.ds(k0, KT)], ds)
            dv[pl.ds(k0, KT), :] = dv_t
            dk[pl.ds(k0, KT), :] = dk_t
            return c

        lax.fori_loop(0, live, over_k, 0)
        for h in range(HEADS):
            back = dqt[h, :, pl.ds(q0, QT)].T
            for b in range(qb):
                dst = pl.multiple_of(meta[0, j * qb + b] * HALF, HALF)
                dq_ref[pl.ds(dst, HALF), h * HD:(h + 1) * HD] = back[b * HALF:(b + 1) * HALF]
        return c

    lax.fori_loop(0, rows_q // QT, over_q, 0)

    if last:
        def spread_k(s, c):
            dst = pl.multiple_of(meta[2, s] * HALF, HALF)
            src = pl.multiple_of(s * HALF, HALF)
            dkv_ref[pl.ds(dst, HALF), :HD] = dk[pl.ds(src, HALF), :].astype(jnp.bfloat16)
            dkv_ref[pl.ds(dst, HALF), HD:] = dv[pl.ds(src, HALF), :].astype(jnp.bfloat16)
            return c

        lax.fori_loop(0, nbk, spread_k, 0, unroll=4)
    else:
        dkv_ref[:, :HD] = dk[...]
        dkv_ref[:, HD:] = dv[...]


def tile_grads(first, last, meta, qg, kv, posq, posk, dkv_in=None):
    rows_q = qg.shape[0]
    rows_k = kv.shape[0]
    vmem = pl.BlockSpec(memory_space=pltpu.VMEM)
    args = [meta, qg, kv, posq, posk] + ([] if first else [dkv_in])
    bf, f32 = jnp.bfloat16, jnp.float32

    def body(*refs):
        tile_kernel(first, last, *refs)

    return pl.pallas_call(
        body,
        out_shape=(
            jax.ShapeDtypeStruct((rows_q, HEADS * HD), f32),
            jax.ShapeDtypeStruct((rows_k, 2 * HD), bf if last else f32),
        ),
        in_specs=[pl.BlockSpec(memory_space=pltpu.SMEM)] + [vmem] * (len(args) - 1),
        out_specs=(vmem, vmem),
        scratch_shapes=[
            pltpu.VMEM((HEADS, rows_q, HD), bf),
            pltpu.VMEM((HEADS, rows_q, HD), bf),
            pltpu.VMEM((rows_q, 128), bf),
            pltpu.VMEM((8, rows_q), f32),
            pltpu.VMEM((8, rows_q), f32),
            pltpu.VMEM((rows_k, HD), bf),
            pltpu.VMEM((rows_k, HD), bf),
            pltpu.VMEM((HD, rows_k), bf),
            pltpu.VMEM((HEADS, HD, rows_q), f32),
            pltpu.VMEM((rows_k, HD), f32),
            pltpu.VMEM((rows_k, HD), f32),
        ],
        compiler_params=pltpu.CompilerParams(vmem_limit_bytes=40 * 1024 * 1024),
        cost_estimate=pl.CostEstimate(
            flops=rows_q * HEADS * rows_k * HD * 5,
            bytes_accessed=4 * 1024 * 1024,
            transcendentals=rows_q * HEADS * rows_k // 2,
        ),
    )(*args)


def in_order(entries):
    n = entries.shape[0]
    rank = jnp.sum((entries[None, :] < entries[:, None]).astype(jnp.int32), axis=1)
    hit = rank[None, :] == jnp.arange(n, dtype=jnp.int32)[:, None]
    place = jnp.arange(n, dtype=jnp.int32)
    order = jnp.sum(jnp.where(hit, place[None, :], 0), axis=1)
    ordered = jnp.sum(jnp.where(hit, entries[None, :], 0), axis=1)
    return order, ordered


def positions(ordered):
    return (ordered[:, None] * HALF + jnp.arange(HALF, dtype=jnp.int32)[None, :]).reshape(-1)


def pack_q_kernel(q_ref, g_ref, lse_ref, delta_ref, out_ref):
    width = HEADS * HD
    out_ref[:, :width] = q_ref[...]
    out_ref[:, width:2 * width] = g_ref[...]
    rows = q_ref.shape[0]
    lane = lax.broadcasted_iota(jnp.int32, (rows, 128), 1)
    which = lane % (2 * HEADS)
    x = jnp.zeros((rows, 128), jnp.float32)
    for h in range(HEADS):
        x = jnp.where(which == h, lse_ref[:, h:h + 1], x)
        x = jnp.where(which == HEADS + h, delta_ref[:, h:h + 1], x)
    out = jnp.zeros((rows, 128), jnp.float32)
    for k in range(PIECES):
        part = x.astype(jnp.bfloat16).astype(jnp.float32)
        x = x - part
        out = jnp.where(lane // (2 * HEADS) == k, part, out)
    out_ref[:, 2 * width:] = out.astype(jnp.bfloat16)


def pack_q(queries, out_grad, log_sum, delta):
    vmem = pl.BlockSpec(memory_space=pltpu.VMEM)
    return pl.pallas_call(
        pack_q_kernel,
        out_shape=jax.ShapeDtypeStruct((queries.shape[0], 2 * HEADS * HD + 128), jnp.bfloat16),
        in_specs=[vmem] * 4,
        out_specs=vmem,
    )(queries, out_grad, log_sum, delta)


def from_offset(x, axes, index_of, d):
    return lax.ppermute(x, axes, [(index_of(j), index_of((j + d) % 4)) for j in range(4)])


def along_x(j):
    return j


def along_y(j):
    return (j % 2) * 2 + j // 2


def back_from(table, index, axis):
    table = jnp.concatenate([lax.slice_in_dim(table, 0, 1, axis=axis), jnp.flip(lax.slice_in_dim(table, 1, 4, axis=axis), axis)], axis)
    return lax.dynamic_slice_in_dim(jnp.concatenate([table, table], axis), (4 - index) % 4, 4, axis)


def local(queries, keys, values, out_grad, log_sum, delta, block_table):
    rows = queries.shape[0]
    width = HEADS * HD
    nx, nyl, nz, nyh, nc = (lax.axis_size(a) for a in ("x", "yl", "z", "yh", "core"))
    ix, iyl, iz, iyh, ic = (lax.axis_index(a) for a in ("x", "yl", "z", "yh", "core"))
    iy = iyh * nyl + iyl
    xy = nx * nyl * nyh
    Y = ("yl", "yh")

    kv = jnp.concatenate([keys, values], axis=1)
    kv = lax.all_to_all(
        jnp.broadcast_to(kv[None], (nz,) + kv.shape), "z", split_axis=0, concat_axis=0, tiled=True
    ).reshape(nz * rows, 2 * HD)

    packed = pack_q(queries, out_grad, log_sum, delta)
    row = jnp.concatenate([packed] + [from_offset(packed, "x", along_x, d) for d in (1, 2, 3)], axis=0)
    q_own = jnp.concatenate([row] + [from_offset(row, Y, along_y, d) for d in (1, 2, 3)], axis=0)
    q_sib = lax.ppermute(q_own, "core", [(0, 1), (1, 0)])

    q_table = block_table.reshape(nx, nyl, nz, nyh, nc, 2)
    q_table = lax.dynamic_index_in_dim(q_table, iz, 2, keepdims=False)
    q_table = q_table.transpose(2, 1, 0, 3, 4).reshape(nyh * nyl, nx, nc, 2)
    q_table = back_from(back_from(q_table, iy, 0), ix, 1)
    k_table = block_table.reshape(nz, nyh, nc, nx, nyl, 2)
    for axis, index in ((1, iyh), (1, ic), (1, ix), (1, iyl)):
        k_table = lax.dynamic_index_in_dim(k_table, index, axis, keepdims=False)
    order_k, sorted_k = in_order(k_table.reshape(-1))
    posk = positions(sorted_k)[:, None]
    metas, posqs = [], []
    for c in (ic, nc - 1 - ic):
        table = lax.dynamic_index_in_dim(q_table, c, 2, keepdims=False).reshape(-1)
        order_q, sorted_q = in_order(table)
        metas.append(jnp.stack([order_q, sorted_q, order_k, sorted_k]))
        posqs.append(positions(sorted_q)[None, :])

    dq_own, dkv = tile_grads(True, False, metas[0], q_own, kv, posqs[0], posk)
    dq_sib, dkv = tile_grads(False, True, metas[1], q_sib, kv, posqs[1], posk, dkv)

    dkv_in = lax.all_to_all(dkv.reshape(nz, rows, 2 * HD), "z", split_axis=0, concat_axis=0, tiled=True)
    dq = dq_own + lax.ppermute(dq_sib, "core", [(0, 1), (1, 0)])
    dq = dq.reshape(nyl * nyh, nx * rows, width)
    far = dq.astype(jnp.bfloat16)
    total = dq[0]
    for d in (1, 2, 3):
        total = total + from_offset(far[d], Y, along_y, 4 - d).astype(jnp.float32)
    dq = total.reshape(nx, rows, width)
    total = dq[0]
    for d in (1, 2, 3):
        total = total + from_offset(dq[d], "x", along_x, 4 - d)
    q_grad = (total * SCALE).astype(jnp.bfloat16)
    dkv_sum = jnp.sum(dkv_in.astype(jnp.float32), axis=0)
    k_grad = (dkv_sum[:, :HD] * SCALE).astype(jnp.bfloat16)
    v_grad = dkv_sum[:, HD:].astype(jnp.bfloat16)
    return (q_grad, k_grad, v_grad)


def solution(mesh):
    fine = Mesh(mesh.devices.reshape(4, 2, 16, 2, 2), ("x", "yl", "z", "yh", "core"))
    q_rows = P(("x", "yl", "z", "yh", "core"), None)
    k_rows = P(("z", "yh", "core", "x", "yl"), None)
    return jax.shard_map(
        local,
        mesh=fine,
        in_specs=(q_rows, k_rows, k_rows, q_rows, q_rows, q_rows, P()),
        out_specs=(q_rows, k_rows, k_rows),
        check_vma=False,
    )
```

```python
import jax
import jax.numpy as jnp
from jax import lax
from jax.experimental import pallas as pl
from jax.experimental.pallas import tpu as pltpu
from jax.sharding import Mesh, PartitionSpec as P

HEADS = 2
HD = 128
HALF = 32
SCALE = HD ** (-0.5)
LOG2E = 1.4426950408889634
PIECES = 3
STATS = 16
QT = 256
KT = 256
TOGETHER = 2
VMEM = pl.BlockSpec(memory_space=pltpu.VMEM)
SMEM = pl.BlockSpec(memory_space=pltpu.SMEM)


def dot(a, b):
    return jnp.dot(a, b, preferred_element_type=jnp.float32)


def dot_nt(a, b):
    return lax.dot_general(a, b, (((1,), (1,)), ((), ())), preferred_element_type=jnp.float32)


def tile_kernel(rank_q, order_q, sorted_q, rank_k, sorted_k, *refs):
    q_refs = refs[:4]
    kv_refs = refs[4:6]
    posq_ref, near_ref, far_ref, own_ref, sib_ref = refs[6:11]
    qs, gs, rows, ks, vs, kt, dqt, dk, dv, todo = refs[11:]
    n_q = qs.shape[0]
    n_k = ks.shape[0]
    per_q = QT // HALF
    per_k = KT // HALF
    part_q = (q_refs[0].shape[0] - STATS) // HALF
    part_k = kv_refs[0].shape[0] // HALF

    for a in range(4):
        for b in range(part_q):
            place = rank_q[a * part_q + b]
            j = place // per_q
            r = pl.multiple_of(place % per_q * HALF, HALF)
            cut = slice(b * HALF, (b + 1) * HALF)
            for h in range(HEADS):
                qs[j, pl.ds(h * QT + r, HALF), :] = q_refs[a][cut, h * HD:(h + 1) * HD]
                gs[j, pl.ds(h * QT + r, HALF), :] = q_refs[a][cut, (HEADS + h) * HD:(HEADS + h + 1) * HD]
    for a in range(2):
        for b in range(part_k):
            place = rank_k[a * part_k + b]
            i = place // per_k
            r = pl.multiple_of(place % per_k * HALF, HALF)
            cut = slice(b * HALF, (b + 1) * HALF)
            ks[i, pl.ds(r, HALF), :] = kv_refs[a][cut, :HD]
            vs[i, pl.ds(r, HALF), :] = kv_refs[a][cut, HD:]

    stat_refs = rows.at[pl.ds(n_q, 4)]
    base = q_refs[0].shape[0] - STATS
    for a in range(4):
        stat_refs[a] = q_refs[a][base:, :].astype(jnp.float32)
    quarter = lax.broadcasted_iota(jnp.int32, (STATS, 128), 1) // HALF
    for t in range(n_q * QT // 128):
        line = jnp.zeros((STATS, 128), jnp.float32)
        for u in range(4):
            b = order_q[t * 4 + u]
            column = pl.multiple_of(b % part_q // 2 * 128, 128)
            piece = rows[n_q + b // part_q, :, pl.ds(column, 128)]
            piece = pltpu.roll(piece, (u - b % 2 + 4) % 4 * HALF, 1)
            line = jnp.where(quarter == u, piece, line)
        j, c = t // (QT // 128), t % (QT // 128)
        n = 2 * HEADS
        stat = line[:n] + line[n:2 * n] + line[2 * n:3 * n]
        for h in range(HEADS):
            cut = slice(h * QT + c * 128, h * QT + (c + 1) * 128)
            rows[j, 0:1, cut] = stat[h:h + 1] * LOG2E
            rows[j, 1:2, cut] = stat[HEADS + h:HEADS + h + 1]

    for i in range(n_k):
        kt[i] = ks[i].astype(jnp.float32).T.astype(jnp.bfloat16)

    dk[...] = jnp.zeros_like(dk)
    dv[...] = jnp.zeros_like(dv)
    dqt[...] = jnp.zeros_like(dqt)

    count = jnp.int32(0)
    dead = jnp.int32(0)
    for j in range(n_q):
        top = sorted_q[j * per_q + per_q - 1]
        for i in range(n_k):
            live = sorted_k[i * per_k] <= top
            todo[count] = jnp.int32(j * n_k + i)
            count = count + live.astype(jnp.int32)
            dead = jnp.where(live, dead, j * n_k + i)
    for u in range(TOGETHER - 1):
        todo[count + u] = dead

    within = lax.broadcasted_iota(jnp.int32, (HALF, 128), 0)

    def one(t):
        j = todo[t] // n_k
        i = todo[t] % n_k
        q, g, k, v = qs[j], gs[j], ks[i], vs[i]
        posk = jnp.concatenate([within + sorted_k[i * per_k + b] * HALF for b in range(per_k)], axis=0)
        posk = jnp.concatenate([posk] * (HEADS * QT // 128), axis=1)
        s = dot_nt(k, q)
        p = jnp.where(posk <= posq_ref[j], jnp.exp2(s * (SCALE * LOG2E) - rows[j, 0:1, :]), 0.0)
        dp = dot_nt(v, g)
        ds = (p * (dp - rows[j, 1:2, :])).astype(jnp.bfloat16)
        dv[i] += dot(p.astype(jnp.bfloat16), g)
        dk[i] += dot(ds, q)
        dqt[j] += dot(kt[i], ds)

    def some(t, c):
        for u in range(TOGETHER):
            one(t * TOGETHER + u)
        return c

    lax.fori_loop(0, (count + TOGETHER - 1) // TOGETHER, some, 0)

    for j in range(n_q):
        for h in range(HEADS):
            back = dqt[j, :, h * QT:(h + 1) * QT].T
            half = back.astype(jnp.bfloat16)
            for b in range(per_q):
                to = order_q[j * per_q + b]
                cut = slice(b * HALF, (b + 1) * HALF)
                lane = slice(h * HD, (h + 1) * HD)
                dst = pl.multiple_of(to * HALF, HALF)
                far_ref[pl.ds(dst, HALF), lane] = half[cut]

                @pl.when(to < part_q)
                def _():
                    near_ref[pl.ds(dst, HALF), lane] = back[cut]
    for a in range(2):
        for b in range(part_k):
            place = rank_k[a * part_k + b]
            i = place // per_k
            r = pl.multiple_of(place % per_k * HALF, HALF)
            cut = slice(b * HALF, (b + 1) * HALF)
            out = own_ref if a == 0 else sib_ref
            out[cut, :HD] = dk[i, pl.ds(r, HALF), :].astype(out.dtype)
            out[cut, HD:] = dv[i, pl.ds(r, HALF), :].astype(out.dtype)


def tile_grads(q_parts, kv_parts, table_q, table_k):
    part = q_parts[0].shape[0] - STATS
    rows_q = 4 * part
    part_k = kv_parts[0].shape[0]
    rows_k = 2 * part_k
    n_q, n_k = rows_q // QT, rows_k // KT
    rank_q, order_q, sorted_q = in_order(table_q)
    rank_k, _, sorted_k = in_order(table_k)
    posq = positions(sorted_q).reshape(n_q, 1, QT)
    posq = jnp.concatenate([posq] * HEADS, axis=2)
    bf, f32 = jnp.bfloat16, jnp.float32
    return pl.pallas_call(
        tile_kernel,
        out_shape=(
            jax.ShapeDtypeStruct((part, HEADS * HD), f32),
            jax.ShapeDtypeStruct((rows_q, HEADS * HD), bf),
            jax.ShapeDtypeStruct((part_k, 2 * HD), f32),
            jax.ShapeDtypeStruct((part_k, 2 * HD), bf),
        ),
        in_specs=[SMEM] * 5 + [VMEM] * 7,
        out_specs=(VMEM,) * 4,
        scratch_shapes=[
            pltpu.VMEM((n_q, HEADS * QT, HD), bf),
            pltpu.VMEM((n_q, HEADS * QT, HD), bf),
            pltpu.VMEM((n_q + 4, STATS, HEADS * QT), f32),
            pltpu.VMEM((n_k, KT, HD), bf),
            pltpu.VMEM((n_k, KT, HD), bf),
            pltpu.VMEM((n_k, HD, KT), bf),
            pltpu.VMEM((n_q, HD, HEADS * QT), f32),
            pltpu.VMEM((n_k, KT, HD), f32),
            pltpu.VMEM((n_k, KT, HD), f32),
            pltpu.SMEM((n_q * n_k + TOGETHER,), jnp.int32),
        ],
        compiler_params=pltpu.CompilerParams(vmem_limit_bytes=40 * 1024 * 1024),
        cost_estimate=pl.CostEstimate(
            flops=rows_q * HEADS * rows_k * HD * 5,
            bytes_accessed=4 * 1024 * 1024,
            transcendentals=rows_q * HEADS * rows_k // 2,
        ),
    )(rank_q, order_q, sorted_q, rank_k, sorted_k, *q_parts, *kv_parts, posq)


def in_order(entries):
    n = entries.shape[0]
    rank = jnp.sum((entries[None, :] < entries[:, None]).astype(jnp.int32), axis=1)
    hit = rank[None, :] == jnp.arange(n, dtype=jnp.int32)[:, None]
    place = jnp.arange(n, dtype=jnp.int32)
    order = jnp.sum(jnp.where(hit, place[None, :], 0), axis=1)
    ordered = jnp.sum(jnp.where(hit, entries[None, :], 0), axis=1)
    return rank, order, ordered


def positions(ordered):
    return (ordered[:, None] * HALF + jnp.arange(HALF, dtype=jnp.int32)[None, :]).reshape(-1)


def pack_kv_kernel(k_ref, v_ref, out_ref):
    for n in range(out_ref.shape[0]):
        out_ref[n, :, :HD] = k_ref[...]
        out_ref[n, :, HD:] = v_ref[...]


def pack_kv(keys, values, copies):
    return pl.pallas_call(
        pack_kv_kernel,
        out_shape=jax.ShapeDtypeStruct((copies, keys.shape[0], 2 * HD), keys.dtype),
        in_specs=[VMEM] * 2,
        out_specs=VMEM,
    )(keys, values)


def pack_q_kernel(q_ref, g_ref, lse_ref, delta_ref, out_ref, wide):
    width = HEADS * HD
    rows = q_ref.shape[0]
    out_ref[:rows, :width] = q_ref[...]
    out_ref[:rows, width:] = g_ref[...]
    out_ref[rows:, :] = jnp.zeros((STATS, 2 * width), jnp.bfloat16)
    wide[...] = jnp.zeros_like(wide)
    n = 2 * HEADS
    for k in range(PIECES):
        wide[k * n:k * n + HEADS, :rows] = lse_ref[...]
        wide[k * n + HEADS:(k + 1) * n, :rows] = delta_ref[...]
    x = wide[...]
    piece = lax.broadcasted_iota(jnp.int32, x.shape, 0) // n
    out = jnp.zeros_like(x)
    for k in range(PIECES):
        part = x.astype(jnp.bfloat16).astype(jnp.float32)
        x = x - part
        out = jnp.where(piece == k, part, out)
    out_ref[rows:, :128] = out.astype(jnp.bfloat16)


def pack_q(queries, out_grad, log_sum, delta):
    rows = queries.shape[0]
    return pl.pallas_call(
        pack_q_kernel,
        out_shape=jax.ShapeDtypeStruct((rows + STATS, 2 * HEADS * HD), jnp.bfloat16),
        in_specs=[VMEM] * 4,
        out_specs=VMEM,
        scratch_shapes=[pltpu.VMEM((STATS, 128), jnp.float32)],
    )(queries, out_grad, log_sum.T, delta.T)


def join_kernel(*refs):
    parts, out_ref = refs[:-1], refs[-1]
    rows = parts[0].shape[0] - STATS
    for a, part in enumerate(parts):
        out_ref[a * rows:(a + 1) * rows, :] = part[:rows, :]
        out_ref[len(parts) * rows:, a * 128:(a + 1) * 128] = part[rows:, :128]


def join(parts):
    rows, width = parts[0].shape
    return pl.pallas_call(
        join_kernel,
        out_shape=jax.ShapeDtypeStruct((len(parts) * (rows - STATS) + STATS, width), parts[0].dtype),
        in_specs=[VMEM] * len(parts),
        out_specs=VMEM,
    )(*parts)


def finish_kv_kernel(in_ref, k_ref, v_ref):
    total = in_ref[0].astype(jnp.float32)
    for n in range(1, in_ref.shape[0]):
        total = total + in_ref[n].astype(jnp.float32)
    k_ref[...] = (total[:, :HD] * SCALE).astype(k_ref.dtype)
    v_ref[...] = total[:, HD:].astype(v_ref.dtype)


def finish_kv(x):
    out = jax.ShapeDtypeStruct((x.shape[1], HD), jnp.bfloat16)
    return pl.pallas_call(
        finish_kv_kernel, out_shape=(out, out), in_specs=[VMEM], out_specs=(VMEM, VMEM)
    )(x)


def from_offset(x, axes, index_of, d):
    return lax.ppermute(x, axes, [(index_of(j), index_of((j + d) % 4)) for j in range(4)])


def along_x(j):
    return j


def along_y(j):
    return (j % 2) * 2 + j // 2


def other_core(x):
    return lax.ppermute(x, "core", [(0, 1), (1, 0)])


def back_from(table, index, axis):
    head = lax.slice_in_dim(table, 0, 1, axis=axis)
    tail = jnp.flip(lax.slice_in_dim(table, 1, 4, axis=axis), axis)
    return lax.dynamic_slice_in_dim(jnp.concatenate([head, tail, head, tail], axis), (4 - index) % 4, 4, axis)


def pick(table, *choices):
    for axis, index in choices:
        table = lax.dynamic_index_in_dim(table, index, axis, keepdims=False)
    return table


def local(queries, keys, values, out_grad, log_sum, delta, block_table):
    rows = queries.shape[0]
    width = HEADS * HD
    nx, nyl, nz, nyh, nc = (lax.axis_size(a) for a in ("x", "yl", "z", "yh", "core"))
    ix, iyl, iz, iyh, ic = (lax.axis_index(a) for a in ("x", "yl", "z", "yh", "core"))
    iy = iyh * nyl + iyl
    y = ("yl", "yh")

    kv_own = lax.all_to_all(pack_kv(keys, values, nz), "z", split_axis=0, concat_axis=0, tiled=True)
    kv_own = kv_own.reshape(nz * rows, 2 * HD)
    kv_sib = other_core(kv_own)
    packed = pack_q(queries, out_grad, log_sum, delta)
    row = join([packed] + [from_offset(packed, "x", along_x, d) for d in (1, 2, 3)])
    q_parts = [row] + [from_offset(row, y, along_y, d) for d in (1, 2, 3)]

    table_q = pick(block_table.reshape(nx, nyl, nz, nyh, nc, 2), (2, iz), (3, ic))
    table_q = table_q.transpose(2, 1, 0, 3).reshape(nyh * nyl, nx, 2)
    table_q = back_from(back_from(table_q, iy, 0), ix, 1).reshape(-1)
    table_k = pick(block_table.reshape(nz, nyh, nc, nx, nyl, 2), (1, iyh), (2, ix), (2, iyl))
    table_k = jnp.concatenate([pick(table_k, (1, c)).reshape(-1) for c in (ic, nc - 1 - ic)])

    near, far, dkv_own, dkv_sib = tile_grads(q_parts, [kv_own, kv_sib], table_q, table_k)

    dkv = (dkv_own + other_core(dkv_sib).astype(jnp.float32)).astype(jnp.bfloat16)
    dkv = lax.all_to_all(dkv.reshape(nz, rows, 2 * HD), "z", split_axis=0, concat_axis=0, tiled=True)
    far = far.reshape(nyl * nyh, nx * rows, width)
    for d in (1, 2, 3):
        near = near + from_offset(far[d], y, along_y, 4 - d).astype(jnp.float32)
    near = near.reshape(nx, rows, width)
    total = near[0]
    for d in (1, 2, 3):
        total = total + from_offset(near[d], "x", along_x, 4 - d)
    q_grad = (total * SCALE).astype(jnp.bfloat16)
    k_grad, v_grad = finish_kv(dkv)
    return (q_grad, k_grad, v_grad)


def solution(mesh):
    fine = Mesh(mesh.devices.reshape(4, 2, 16, 2, 2), ("x", "yl", "z", "yh", "core"))
    q_rows = P(("x", "yl", "z", "yh", "core"), None)
    k_rows = P(("z", "yh", "core", "x", "yl"), None)
    return jax.shard_map(
        local,
        mesh=fine,
        in_specs=(q_rows, k_rows, k_rows, q_rows, q_rows, q_rows, P()),
        out_specs=(q_rows, k_rows, k_rows),
        check_vma=False,
    )
```

```python
import jax
import jax.numpy as jnp
from jax import lax
from jax.experimental import pallas as pl
from jax.experimental.pallas import tpu as pltpu
from jax.sharding import Mesh, PartitionSpec as P

HEADS = 2
HD = 128
HALF = 32
SCALE = HD ** (-0.5)
LOG2E = 1.4426950408889634
PIECES = 3
STATS = 16
QT = 256
KT = 256
TOGETHER = 2
VMEM = pl.BlockSpec(memory_space=pltpu.VMEM)
SMEM = pl.BlockSpec(memory_space=pltpu.SMEM)


def dot(a, b):
    return jnp.dot(a, b, preferred_element_type=jnp.float32)


def dot_nt(a, b):
    return lax.dot_general(a, b, (((1,), (1,)), ((), ())), preferred_element_type=jnp.float32)


def tile_kernel(rank_q, order_q, sorted_q, rank_k, sorted_k, *refs):
    q_refs = refs[:4]
    kv_refs = refs[4:6]
    posq_ref, near_ref, far_ref, own_ref, sib_ref = refs[6:11]
    qs, gs, rows, ks, vs, kt, dqt, dk, dv, todo = refs[11:]
    n_q = qs.shape[0]
    n_k = ks.shape[0]
    per_q = QT // HALF
    per_k = KT // HALF
    part_q = (q_refs[0].shape[0] - STATS) // HALF
    part_k = kv_refs[0].shape[0] // HALF

    for a in range(4):
        for b in range(part_q):
            place = rank_q[a * part_q + b]
            j = place // per_q
            r = pl.multiple_of(place % per_q * HALF, HALF)
            cut = slice(b * HALF, (b + 1) * HALF)
            for h in range(HEADS):
                qs[j, pl.ds(h * QT + r, HALF), :] = q_refs[a][cut, h * HD:(h + 1) * HD]
                gs[j, pl.ds(h * QT + r, HALF), :] = q_refs[a][cut, (HEADS + h) * HD:(HEADS + h + 1) * HD]
    for a in range(2):
        for b in range(part_k):
            place = rank_k[a * part_k + b]
            i = place // per_k
            r = pl.multiple_of(place % per_k * HALF, HALF)
            cut = slice(b * HALF, (b + 1) * HALF)
            ks[i, pl.ds(r, HALF), :] = kv_refs[a][cut, :HD]
            vs[i, pl.ds(r, HALF), :] = kv_refs[a][cut, HD:]

    stat_refs = rows.at[pl.ds(n_q, 4)]
    base = q_refs[0].shape[0] - STATS
    for a in range(4):
        stat_refs[a] = q_refs[a][base:, :].astype(jnp.float32)
    quarter = lax.broadcasted_iota(jnp.int32, (STATS, 128), 1) // HALF
    for t in range(n_q * QT // 128):
        line = jnp.zeros((STATS, 128), jnp.float32)
        for u in range(4):
            b = order_q[t * 4 + u]
            column = pl.multiple_of(b % part_q // 2 * 128, 128)
            piece = rows[n_q + b // part_q, :, pl.ds(column, 128)]
            piece = pltpu.roll(piece, (u - b % 2 + 4) % 4 * HALF, 1)
            line = jnp.where(quarter == u, piece, line)
        j, c = t // (QT // 128), t % (QT // 128)
        n = 2 * HEADS
        stat = line[:n] + line[n:2 * n] + line[2 * n:3 * n]
        for h in range(HEADS):
            cut = slice(h * QT + c * 128, h * QT + (c + 1) * 128)
            rows[j, 0:1, cut] = stat[h:h + 1] * LOG2E
            rows[j, 1:2, cut] = stat[HEADS + h:HEADS + h + 1]

    for i in range(n_k):
        kt[i] = ks[i].astype(jnp.float32).T.astype(jnp.bfloat16)

    dk[...] = jnp.zeros_like(dk)
    dv[...] = jnp.zeros_like(dv)
    dqt[...] = jnp.zeros_like(dqt)

    count = jnp.int32(0)
    dead = jnp.int32(0)
    for j in range(n_q):
        top = sorted_q[j * per_q + per_q - 1]
        for i in range(n_k):
            live = sorted_k[i * per_k] <= top
            todo[count] = jnp.int32(j * n_k + i)
            count = count + live.astype(jnp.int32)
            dead = jnp.where(live, dead, j * n_k + i)
    for u in range(TOGETHER - 1):
        todo[count + u] = dead

    within = lax.broadcasted_iota(jnp.int32, (HALF, 128), 0)

    def one(t):
        j = todo[t] // n_k
        i = todo[t] % n_k
        q, g, k, v = qs[j], gs[j], ks[i], vs[i]
        posk = jnp.concatenate([within + sorted_k[i * per_k + b] * HALF for b in range(per_k)], axis=0)
        posk = jnp.concatenate([posk] * (HEADS * QT // 128), axis=1)
        s = dot_nt(k, q)
        p = jnp.where(posk <= posq_ref[j], jnp.exp2(s * (SCALE * LOG2E) - rows[j, 0:1, :]), 0.0)
        dp = dot_nt(v, g)
        ds = (p * (dp - rows[j, 1:2, :])).astype(jnp.bfloat16)
        dv[i] += dot(p.astype(jnp.bfloat16), g)
        dk[i] += dot(ds, q)
        dqt[j] += dot(kt[i], ds)

    def some(t, c):
        for u in range(TOGETHER):
            one(t * TOGETHER + u)
        return c

    lax.fori_loop(0, (count + TOGETHER - 1) // TOGETHER, some, 0)

    for j in range(n_q):
        for h in range(HEADS):
            back = dqt[j, :, h * QT:(h + 1) * QT].T
            half = back.astype(jnp.bfloat16)
            for b in range(per_q):
                to = order_q[j * per_q + b]
                cut = slice(b * HALF, (b + 1) * HALF)
                lane = slice(h * HD, (h + 1) * HD)
                dst = pl.multiple_of(to * HALF, HALF)
                far_ref[pl.ds(dst, HALF), lane] = half[cut]

                @pl.when(to < part_q)
                def _():
                    near_ref[pl.ds(dst, HALF), lane] = back[cut]
    for a in range(2):
        for b in range(part_k):
            place = rank_k[a * part_k + b]
            i = place // per_k
            r = pl.multiple_of(place % per_k * HALF, HALF)
            cut = slice(b * HALF, (b + 1) * HALF)
            out = own_ref if a == 0 else sib_ref
            out[cut, :HD] = dk[i, pl.ds(r, HALF), :].astype(out.dtype)
            out[cut, HD:] = dv[i, pl.ds(r, HALF), :].astype(out.dtype)


def tile_grads(q_parts, kv_parts, table_q, table_k):
    part = q_parts[0].shape[0] - STATS
    rows_q = 4 * part
    part_k = kv_parts[0].shape[0]
    rows_k = 2 * part_k
    n_q, n_k = rows_q // QT, rows_k // KT
    rank_q, order_q, sorted_q = in_order(table_q)
    rank_k, _, sorted_k = in_order(table_k)
    posq = positions(sorted_q).reshape(n_q, 1, QT)
    posq = jnp.concatenate([posq] * HEADS, axis=2)
    bf, f32 = jnp.bfloat16, jnp.float32
    return pl.pallas_call(
        tile_kernel,
        out_shape=(
            jax.ShapeDtypeStruct((part, HEADS * HD), f32),
            jax.ShapeDtypeStruct((rows_q, HEADS * HD), bf),
            jax.ShapeDtypeStruct((part_k, 2 * HD), f32),
            jax.ShapeDtypeStruct((part_k, 2 * HD), bf),
        ),
        in_specs=[SMEM] * 5 + [VMEM] * 7,
        out_specs=(VMEM,) * 4,
        scratch_shapes=[
            pltpu.VMEM((n_q, HEADS * QT, HD), bf),
            pltpu.VMEM((n_q, HEADS * QT, HD), bf),
            pltpu.VMEM((n_q + 4, STATS, HEADS * QT), f32),
            pltpu.VMEM((n_k, KT, HD), bf),
            pltpu.VMEM((n_k, KT, HD), bf),
            pltpu.VMEM((n_k, HD, KT), bf),
            pltpu.VMEM((n_q, HD, HEADS * QT), f32),
            pltpu.VMEM((n_k, KT, HD), f32),
            pltpu.VMEM((n_k, KT, HD), f32),
            pltpu.SMEM((n_q * n_k + TOGETHER,), jnp.int32),
        ],
        compiler_params=pltpu.CompilerParams(vmem_limit_bytes=40 * 1024 * 1024),
        cost_estimate=pl.CostEstimate(
            flops=rows_q * HEADS * rows_k * HD * 5,
            bytes_accessed=4 * 1024 * 1024,
            transcendentals=rows_q * HEADS * rows_k // 2,
        ),
    )(rank_q, order_q, sorted_q, rank_k, sorted_k, *q_parts, *kv_parts, posq)


def in_order(entries):
    n = entries.shape[0]
    rank = jnp.sum((entries[None, :] < entries[:, None]).astype(jnp.int32), axis=1)
    hit = rank[None, :] == jnp.arange(n, dtype=jnp.int32)[:, None]
    place = jnp.arange(n, dtype=jnp.int32)
    order = jnp.sum(jnp.where(hit, place[None, :], 0), axis=1)
    ordered = jnp.sum(jnp.where(hit, entries[None, :], 0), axis=1)
    return rank, order, ordered


def positions(ordered):
    return (ordered[:, None] * HALF + jnp.arange(HALF, dtype=jnp.int32)[None, :]).reshape(-1)


def pack_kv_kernel(k_ref, v_ref, out_ref):
    for n in range(out_ref.shape[0]):
        out_ref[n, :, :HD] = k_ref[...]
        out_ref[n, :, HD:] = v_ref[...]


def pack_kv(keys, values, copies):
    return pl.pallas_call(
        pack_kv_kernel,
        out_shape=jax.ShapeDtypeStruct((copies, keys.shape[0], 2 * HD), keys.dtype),
        in_specs=[VMEM] * 2,
        out_specs=VMEM,
    )(keys, values)


def pack_q_kernel(q_ref, g_ref, lse_ref, delta_ref, out_ref, wide):
    width = HEADS * HD
    rows = q_ref.shape[0]
    out_ref[:rows, :width] = q_ref[...]
    out_ref[:rows, width:] = g_ref[...]
    out_ref[rows:, :] = jnp.zeros((STATS, 2 * width), jnp.bfloat16)
    wide[...] = jnp.zeros_like(wide)
    n = 2 * HEADS
    for k in range(PIECES):
        wide[k * n:k * n + HEADS, :rows] = lse_ref[...]
        wide[k * n + HEADS:(k + 1) * n, :rows] = delta_ref[...]
    x = wide[...]
    piece = lax.broadcasted_iota(jnp.int32, x.shape, 0) // n
    out = jnp.zeros_like(x)
    for k in range(PIECES):
        part = x.astype(jnp.bfloat16).astype(jnp.float32)
        x = x - part
        out = jnp.where(piece == k, part, out)
    out_ref[rows:, :128] = out.astype(jnp.bfloat16)


def pack_q(queries, out_grad, log_sum, delta):
    rows = queries.shape[0]
    return pl.pallas_call(
        pack_q_kernel,
        out_shape=jax.ShapeDtypeStruct((rows + STATS, 2 * HEADS * HD), jnp.bfloat16),
        in_specs=[VMEM] * 4,
        out_specs=VMEM,
        scratch_shapes=[pltpu.VMEM((STATS, 128), jnp.float32)],
    )(queries, out_grad, log_sum.T, delta.T)


def join(parts):
    rows = parts[0].shape[0] - STATS
    stats = jnp.concatenate([p[rows:, :128] for p in parts], axis=1)
    return jnp.concatenate([p[:rows] for p in parts] + [stats], axis=0)


def from_offset(x, stage, d):
    pairs = []
    for ix in range(4):
        for iy in range(4):
            for core in range(2):
                tx, ty = ((ix + d) % 4, iy) if core == stage else (ix, (iy + d) % 4)
                pairs.append((place(ix, iy, core), place(tx, ty, core)))
    return lax.ppermute(x, ("x", "yl", "yh", "core"), pairs)


def place(ix, iy, core):
    return ((ix * 2 + iy % 2) * 2 + iy // 2) * 2 + core


def other_core(x):
    return lax.ppermute(x, "core", [(0, 1), (1, 0)])


def back_from(table, index, axis):
    head = lax.slice_in_dim(table, 0, 1, axis=axis)
    tail = jnp.flip(lax.slice_in_dim(table, 1, 4, axis=axis), axis)
    return lax.dynamic_slice_in_dim(jnp.concatenate([head, tail, head, tail], axis), (4 - index) % 4, 4, axis)


def pick(table, *choices):
    for axis, index in choices:
        table = lax.dynamic_index_in_dim(table, index, axis, keepdims=False)
    return table


def local(queries, keys, values, out_grad, log_sum, delta, block_table):
    rows = queries.shape[0]
    width = HEADS * HD
    nx, nyl, nz, nyh, nc = (lax.axis_size(a) for a in ("x", "yl", "z", "yh", "core"))
    ix, iyl, iz, iyh, ic = (lax.axis_index(a) for a in ("x", "yl", "z", "yh", "core"))
    iy = iyh * nyl + iyl

    kv_own = lax.all_to_all(pack_kv(keys, values, nz), "z", split_axis=0, concat_axis=0, tiled=True)
    kv_own = kv_own.reshape(nz * rows, 2 * HD)
    packed = pack_q(queries, out_grad, log_sum, delta)
    line = join([packed] + [from_offset(packed, 0, d) for d in (1, 2, 3)])
    q_parts = [line] + [from_offset(line, 1, d) for d in (1, 2, 3)]
    kv_own, q_parts = lax.optimization_barrier((kv_own, q_parts))
    kv_sib = other_core(kv_own)

    table_q = pick(block_table.reshape(nx, nyl, nz, nyh, nc, 2), (2, iz), (3, ic))
    table_q = table_q.transpose(0, 2, 1, 3).reshape(nx, nyh * nyl, 2)
    table_q = back_from(back_from(table_q, ix, 0), iy, 1)
    table_q = jnp.where(ic == 0, table_q.transpose(1, 0, 2), table_q).reshape(-1)
    table_k = pick(block_table.reshape(nz, nyh, nc, nx, nyl, 2), (1, iyh), (2, ix), (2, iyl))
    table_k = jnp.concatenate([pick(table_k, (1, c)).reshape(-1) for c in (ic, nc - 1 - ic)])

    near, far, dkv_own, dkv_sib = tile_grads(q_parts, [kv_own, kv_sib], table_q, table_k)

    dkv = (dkv_own + other_core(dkv_sib).astype(jnp.float32)).astype(jnp.bfloat16)
    dkv = lax.all_to_all(dkv.reshape(nz, rows, 2 * HD), "z", split_axis=0, concat_axis=0, tiled=True)
    far = far.reshape(4, 4 * rows, width)
    for d in (1, 2, 3):
        near = near + from_offset(far[d], 1, 4 - d).astype(jnp.float32)
    near = near.reshape(4, rows, width)
    total = near[0]
    for d in (1, 2, 3):
        total = total + from_offset(near[d], 0, 4 - d)
    q_grad = (total * SCALE).astype(jnp.bfloat16)
    dkv = jnp.sum(dkv.astype(jnp.float32), axis=0)
    k_grad = (dkv[:, :HD] * SCALE).astype(jnp.bfloat16)
    v_grad = dkv[:, HD:].astype(jnp.bfloat16)
    return (q_grad, k_grad, v_grad)


def solution(mesh):
    fine = Mesh(mesh.devices.reshape(4, 2, 16, 2, 2), ("x", "yl", "z", "yh", "core"))
    q_rows = P(("x", "yl", "z", "yh", "core"), None)
    k_rows = P(("z", "yh", "core", "x", "yl"), None)
    return jax.shard_map(
        local,
        mesh=fine,
        in_specs=(q_rows, k_rows, k_rows, q_rows, q_rows, q_rows, P()),
        out_specs=(q_rows, k_rows, k_rows),
        check_vma=False,
    )
```

```python
import jax
import jax.numpy as jnp
from jax import lax
from jax.experimental import pallas as pl
from jax.experimental.pallas import tpu as pltpu
from jax.sharding import Mesh, PartitionSpec as P

HEADS = 2
HD = 128
HALF = 32
SCALE = HD ** (-0.5)
LOG2E = 1.4426950408889634
PIECES = 3
STATS = 16
QT = 256
KT = 256
TOGETHER = 2
VMEM = pl.BlockSpec(memory_space=pltpu.VMEM)
SMEM = pl.BlockSpec(memory_space=pltpu.SMEM)


def dot(a, b):
    return jnp.dot(a, b, preferred_element_type=jnp.float32)


def dot_nt(a, b):
    return lax.dot_general(a, b, (((1,), (1,)), ((), ())), preferred_element_type=jnp.float32)


def tile_kernel(core, rank_q, order_q, sorted_q, rank_k, sorted_k, *refs):
    q_refs = refs[:2]
    kv_refs = refs[2:6]
    posq_ref, dq_ref, near_ref, far_ref = refs[6:10]
    qs, gs, stats, rows, ks, vs, kt, dqt, dk, dv, todo = refs[10:]
    n_q = qs.shape[0]
    n_k = ks.shape[0]
    per_q = QT // HALF
    per_k = KT // HALF
    devs = q_refs[0].shape[0]
    part_q = (q_refs[0].shape[1] - STATS) // HALF
    part_k = kv_refs[0].shape[0] // HALF

    for a in range(2):
        for n in range(devs):
            for b in range(part_q):
                place = rank_q[(a * devs + n) * part_q + b]
                j = place // per_q
                r = pl.multiple_of(place % per_q * HALF, HALF)
                cut = slice(b * HALF, (b + 1) * HALF)
                for h in range(HEADS):
                    qs[j, pl.ds(h * QT + r, HALF), :] = q_refs[a][n, cut, h * HD:(h + 1) * HD]
                    gs[j, pl.ds(h * QT + r, HALF), :] = q_refs[a][n, cut, (HEADS + h) * HD:(HEADS + h + 1) * HD]
            stats[a * devs + n] = q_refs[a][n, part_q * HALF:, :128].astype(jnp.float32)
    for a in range(4):
        for b in range(part_k):
            place = rank_k[a * part_k + b]
            i = place // per_k
            r = pl.multiple_of(place % per_k * HALF, HALF)
            cut = slice(b * HALF, (b + 1) * HALF)
            ks[i, pl.ds(r, HALF), :] = kv_refs[a][cut, :HD]
            vs[i, pl.ds(r, HALF), :] = kv_refs[a][cut, HD:]

    quarter = lax.broadcasted_iota(jnp.int32, (STATS, 128), 1) // HALF
    for t in range(n_q * QT // 128):
        line = jnp.zeros((STATS, 128), jnp.float32)
        for u in range(4):
            b = order_q[t * 4 + u]
            piece = pltpu.roll(stats[b // part_q], (u - b % part_q + 4) % 4 * HALF, 1)
            line = jnp.where(quarter == u, piece, line)
        j, c = t // (QT // 128), t % (QT // 128)
        n = 2 * HEADS
        stat = line[:n] + line[n:2 * n] + line[2 * n:3 * n]
        for h in range(HEADS):
            cut = slice(h * QT + c * 128, h * QT + (c + 1) * 128)
            rows[j, 0:1, cut] = stat[h:h + 1] * LOG2E
            rows[j, 1:2, cut] = stat[HEADS + h:HEADS + h + 1]

    for i in range(n_k):
        kt[i] = ks[i].astype(jnp.float32).T.astype(jnp.bfloat16)

    dk[...] = jnp.zeros_like(dk)
    dv[...] = jnp.zeros_like(dv)
    dqt[...] = jnp.zeros_like(dqt)

    count = jnp.int32(0)
    dead = jnp.int32(0)
    for j in range(n_q):
        top = sorted_q[j * per_q + per_q - 1]
        for i in range(n_k):
            live = sorted_k[i * per_k] <= top
            todo[count] = jnp.int32(j * n_k + i)
            count = count + live.astype(jnp.int32)
            dead = jnp.where(live, dead, j * n_k + i)
    for u in range(TOGETHER - 1):
        todo[count + u] = dead

    within = lax.broadcasted_iota(jnp.int32, (HALF, 128), 0)

    def one(t):
        j = todo[t] // n_k
        i = todo[t] % n_k
        q, g, k, v = qs[j], gs[j], ks[i], vs[i]
        posk = jnp.concatenate([within + sorted_k[i * per_k + b] * HALF for b in range(per_k)], axis=0)
        posk = jnp.concatenate([posk] * (HEADS * QT // 128), axis=1)
        s = dot_nt(k, q)
        p = jnp.where(posk <= posq_ref[j], jnp.exp2(s * (SCALE * LOG2E) - rows[j, 0:1, :]), 0.0)
        dp = dot_nt(v, g)
        ds = (p * (dp - rows[j, 1:2, :])).astype(jnp.bfloat16)
        dv[i] += dot(p.astype(jnp.bfloat16), g)
        dk[i] += dot(ds, q)
        dqt[j] += dot(kt[i], ds)

    def some(t, c):
        for u in range(TOGETHER):
            one(t * TOGETHER + u)
        return c

    lax.fori_loop(0, (count + TOGETHER - 1) // TOGETHER, some, 0)

    half_q = devs * part_q
    for j in range(n_q):
        for h in range(HEADS):
            back = dqt[j, :, h * QT:(h + 1) * QT].T.astype(jnp.bfloat16)
            for b in range(per_q):
                to = order_q[j * per_q + b]
                owner = jnp.where(to < half_q, core[0], 1 - core[0])
                dst = pl.multiple_of((owner * half_q + to % half_q) * HALF, HALF)
                dq_ref[pl.ds(dst, HALF), h * HD:(h + 1) * HD] = back[b * HALF:(b + 1) * HALF]
    for a in range(4):
        for b in range(part_k):
            place = rank_k[a * part_k + b]
            i = place // per_k
            r = pl.multiple_of(place % per_k * HALF, HALF)
            out = near_ref if a == 0 else far_ref
            cut = slice((b if a == 0 else (a - 1) * part_k + b) * HALF, (b + 1 if a == 0 else (a - 1) * part_k + b + 1) * HALF)
            out[cut, :HD] = dk[i, pl.ds(r, HALF), :].astype(out.dtype)
            out[cut, HD:] = dv[i, pl.ds(r, HALF), :].astype(out.dtype)


def tile_grads(core, q_parts, kv_parts, table_q, table_k):
    devs, part = q_parts[0].shape[:2]
    rows_q = 2 * devs * (part - STATS)
    part_k = kv_parts[0].shape[0]
    rows_k = 4 * part_k
    n_q, n_k = rows_q // QT, rows_k // KT
    rank_q, order_q, sorted_q = in_order(table_q)
    rank_k, _, sorted_k = in_order(table_k)
    posq = positions(sorted_q).reshape(n_q, 1, QT)
    posq = jnp.concatenate([posq] * HEADS, axis=2)
    bf, f32 = jnp.bfloat16, jnp.float32
    return pl.pallas_call(
        tile_kernel,
        out_shape=(
            jax.ShapeDtypeStruct((rows_q, HEADS * HD), bf),
            jax.ShapeDtypeStruct((part_k, 2 * HD), f32),
            jax.ShapeDtypeStruct((3 * part_k, 2 * HD), bf),
        ),
        in_specs=[SMEM] * 6 + [VMEM] * 7,
        out_specs=(VMEM,) * 3,
        scratch_shapes=[
            pltpu.VMEM((n_q, HEADS * QT, HD), bf),
            pltpu.VMEM((n_q, HEADS * QT, HD), bf),
            pltpu.VMEM((2 * devs, STATS, 128), f32),
            pltpu.VMEM((n_q, 8, HEADS * QT), f32),
            pltpu.VMEM((n_k, KT, HD), bf),
            pltpu.VMEM((n_k, KT, HD), bf),
            pltpu.VMEM((n_k, HD, KT), bf),
            pltpu.VMEM((n_q, HD, HEADS * QT), f32),
            pltpu.VMEM((n_k, KT, HD), f32),
            pltpu.VMEM((n_k, KT, HD), f32),
            pltpu.SMEM((n_q * n_k + TOGETHER,), jnp.int32),
        ],
        compiler_params=pltpu.CompilerParams(vmem_limit_bytes=40 * 1024 * 1024),
        cost_estimate=pl.CostEstimate(
            flops=rows_q * HEADS * rows_k * HD * 5,
            bytes_accessed=4 * 1024 * 1024,
            transcendentals=rows_q * HEADS * rows_k // 2,
        ),
    )(core, rank_q, order_q, sorted_q, rank_k, sorted_k, *q_parts, *kv_parts, posq)


def in_order(entries):
    n = entries.shape[0]
    rank = jnp.sum((entries[None, :] < entries[:, None]).astype(jnp.int32), axis=1)
    hit = rank[None, :] == jnp.arange(n, dtype=jnp.int32)[:, None]
    place = jnp.arange(n, dtype=jnp.int32)
    order = jnp.sum(jnp.where(hit, place[None, :], 0), axis=1)
    ordered = jnp.sum(jnp.where(hit, entries[None, :], 0), axis=1)
    return rank, order, ordered


def positions(ordered):
    return (ordered[:, None] * HALF + jnp.arange(HALF, dtype=jnp.int32)[None, :]).reshape(-1)


def pack_q_kernel(q_ref, g_ref, lse_ref, delta_ref, out_ref, wide):
    width = HEADS * HD
    rows = q_ref.shape[0]
    out_ref[:rows, :width] = q_ref[...]
    out_ref[:rows, width:] = g_ref[...]
    out_ref[rows:, :] = jnp.zeros((STATS, 2 * width), jnp.bfloat16)
    wide[...] = jnp.zeros_like(wide)
    n = 2 * HEADS
    for k in range(PIECES):
        wide[k * n:k * n + HEADS, :rows] = lse_ref[...]
        wide[k * n + HEADS:(k + 1) * n, :rows] = delta_ref[...]
    x = wide[...]
    piece = lax.broadcasted_iota(jnp.int32, x.shape, 0) // n
    out = jnp.zeros_like(x)
    for k in range(PIECES):
        part = x.astype(jnp.bfloat16).astype(jnp.float32)
        x = x - part
        out = jnp.where(piece == k, part, out)
    out_ref[rows:, :128] = out.astype(jnp.bfloat16)


def pack_q(queries, out_grad, log_sum, delta):
    rows = queries.shape[0]
    return pl.pallas_call(
        pack_q_kernel,
        out_shape=jax.ShapeDtypeStruct((rows + STATS, 2 * HEADS * HD), jnp.bfloat16),
        in_specs=[VMEM] * 4,
        out_specs=VMEM,
        scratch_shapes=[pltpu.VMEM((STATS, 128), jnp.float32)],
    )(queries, out_grad, log_sum.T, delta.T)


FAR = (4, -4, 8)
CLOSE = (1, -1, 2)


def from_far(x, d, back=1):
    return lax.ppermute(x, "z", [(i, (i + back * d) % 16) for i in range(16)])


def from_close(x, d, back=1):
    pairs = []
    for i in range(16):
        for core in range(2):
            step = -d if core == 1 and d == 2 else d
            pairs.append((i * 2 + core, (i + back * step) % 16 * 2 + core))
    return lax.ppermute(x, ("z", "core"), pairs)


def other_core(x):
    return lax.ppermute(x, "core", [(0, 1), (1, 0)])


def look_up(table, index):
    spot = jnp.arange(table.shape[0], dtype=jnp.int32)
    return jnp.sum(jnp.where(index[:, None] == spot[None, :], table[None, :], 0), axis=1)


def both_blocks(device):
    return (2 * device[:, None] + jnp.arange(2, dtype=jnp.int32)[None, :]).reshape(-1)


def local(queries, keys, values, out_grad, log_sum, delta, block_table):
    rows = queries.shape[0]
    width = HEADS * HD
    nx, nyl, nz, nyh, nc = (lax.axis_size(a) for a in ("x", "yl", "z", "yh", "core"))
    ix, iyl, iz, iyh, ic = (lax.axis_index(a) for a in ("x", "yl", "z", "yh", "core"))
    plane = ("x", "yl", "yh")
    devs = nx * nyl * nyh

    packed = pack_q(queries, out_grad, log_sum, delta)
    packed = jnp.broadcast_to(packed[None], (devs,) + packed.shape)
    q_own = lax.all_to_all(packed, plane, split_axis=0, concat_axis=0, tiled=True)
    kv = jnp.concatenate([keys, values], axis=1)
    kv = jnp.concatenate([kv] + [from_far(kv, d) for d in FAR], axis=0)
    kv_parts = [kv] + [from_close(kv, d) for d in CLOSE]
    q_own, kv_parts = lax.optimization_barrier((q_own, kv_parts))
    q_sib = other_core(q_own)

    spot = jnp.arange(devs, dtype=jnp.int32)
    at = [((spot // nyh) * nz + iz) * nyh * nc + (spot % nyh) * nc + c for c in (ic, nc - 1 - ic)]
    table_q = look_up(block_table, both_blocks(jnp.concatenate(at)))
    turn = jnp.where(ic == 1, -1, 1)
    far = jnp.array((0,) + FAR, jnp.int32)
    close = jnp.stack([jnp.int32(0), jnp.int32(1), jnp.int32(-1), 2 * turn])
    z = (iz - close[:, None] - far[None, :]).reshape(-1) % nz
    at = ((z * nyh + iyh) * nc + ic) * nx * nyl + ix * nyl + iyl
    table_k = look_up(block_table, both_blocks(at))

    dq, near, far_kv = tile_grads(ic.reshape(1).astype(jnp.int32), [q_own, q_sib], kv_parts, table_q, table_k)

    dq = dq.reshape(nc * devs, rows, width)
    dq = lax.all_to_all(dq, ("core",) + plane, split_axis=0, concat_axis=0, tiled=True)
    q_grad = (jnp.sum(dq.astype(jnp.float32), axis=0) * SCALE).astype(jnp.bfloat16)
    far_kv = far_kv.reshape(3, 4 * rows, 2 * HD)
    for n, d in enumerate(CLOSE):
        near = near + from_close(far_kv[n], d, -1).astype(jnp.float32)
    near = near.reshape(4, rows, 2 * HD)
    total = near[0]
    for n, d in enumerate(FAR):
        total = total + from_far(near[n + 1], d, -1)
    k_grad = (total[:, :HD] * SCALE).astype(jnp.bfloat16)
    v_grad = total[:, HD:].astype(jnp.bfloat16)
    return (q_grad, k_grad, v_grad)


def solution(mesh):
    fine = Mesh(mesh.devices.reshape(4, 2, 16, 2, 2), ("x", "yl", "z", "yh", "core"))
    q_rows = P(("x", "yl", "z", "yh", "core"), None)
    k_rows = P(("z", "yh", "core", "x", "yl"), None)
    return jax.shard_map(
        local,
        mesh=fine,
        in_specs=(q_rows, k_rows, k_rows, q_rows, q_rows, q_rows, P()),
        out_specs=(q_rows, k_rows, k_rows),
        check_vma=False,
    )
```

```python
import jax
import jax.numpy as jnp
from jax import lax
from jax.experimental import pallas as pl
from jax.experimental.pallas import tpu as pltpu
from jax.sharding import Mesh, PartitionSpec as P

HEADS = 2
HD = 128
HALF = 32
SCALE = HD ** (-0.5)
LOG2E = 1.4426950408889634
PIECES = 3
STATS = 16
QT = 256
KT = 256
TOGETHER = 4
VMEM = pl.BlockSpec(memory_space=pltpu.VMEM)
SMEM = pl.BlockSpec(memory_space=pltpu.SMEM)


def dot(a, b):
    return jnp.dot(a, b, preferred_element_type=jnp.float32)


def dot_nt(a, b):
    return lax.dot_general(a, b, (((1,), (1,)), ((), ())), preferred_element_type=jnp.float32)


def tile_kernel(rank_q, order_q, sorted_q, rank_k, sorted_k, *refs):
    q_refs = refs[:4]
    kv_refs = refs[4:6]
    posq_ref, near_ref, far_ref, own_ref, sib_ref = refs[6:11]
    qs, gs, rows, ks, vs, kt, dqt, dk, dv, todo = refs[11:]
    n_q = qs.shape[0]
    n_k = ks.shape[0]
    per_q = QT // HALF
    per_k = KT // HALF
    part_q = (q_refs[0].shape[0] - STATS) // HALF
    part_k = kv_refs[0].shape[0] // HALF

    for a in range(4):
        for b in range(part_q):
            place = rank_q[a * part_q + b]
            j = place // per_q
            r = pl.multiple_of(place % per_q * HALF, HALF)
            cut = slice(b * HALF, (b + 1) * HALF)
            for h in range(HEADS):
                qs[j, pl.ds(h * QT + r, HALF), :] = q_refs[a][cut, h * HD:(h + 1) * HD]
                gs[j, pl.ds(h * QT + r, HALF), :] = q_refs[a][cut, (HEADS + h) * HD:(HEADS + h + 1) * HD]
    for a in range(2):
        for b in range(part_k):
            place = rank_k[a * part_k + b]
            i = place // per_k
            r = pl.multiple_of(place % per_k * HALF, HALF)
            cut = slice(b * HALF, (b + 1) * HALF)
            ks[i, pl.ds(r, HALF), :] = kv_refs[a][cut, :HD]
            vs[i, pl.ds(r, HALF), :] = kv_refs[a][cut, HD:]

    stat_refs = rows.at[pl.ds(n_q, 4)]
    base = q_refs[0].shape[0] - STATS
    for a in range(4):
        stat_refs[a] = q_refs[a][base:, :].astype(jnp.float32)
    quarter = lax.broadcasted_iota(jnp.int32, (STATS, 128), 1) // HALF
    for t in range(n_q * QT // 128):
        line = jnp.zeros((STATS, 128), jnp.float32)
        for u in range(4):
            b = order_q[t * 4 + u]
            column = pl.multiple_of(b % part_q // 2 * 128, 128)
            piece = rows[n_q + b // part_q, :, pl.ds(column, 128)]
            piece = pltpu.roll(piece, (u - b % 2 + 4) % 4 * HALF, 1)
            line = jnp.where(quarter == u, piece, line)
        j, c = t // (QT // 128), t % (QT // 128)
        n = 2 * HEADS
        stat = line[:n] + line[n:2 * n] + line[2 * n:3 * n]
        for h in range(HEADS):
            cut = slice(h * QT + c * 128, h * QT + (c + 1) * 128)
            rows[j, 0:1, cut] = stat[h:h + 1] * LOG2E
            rows[j, 1:2, cut] = stat[HEADS + h:HEADS + h + 1]

    for i in range(n_k):
        kt[i] = ks[i].astype(jnp.float32).T.astype(jnp.bfloat16)

    dk[...] = jnp.zeros_like(dk)
    dv[...] = jnp.zeros_like(dv)
    dqt[...] = jnp.zeros_like(dqt)

    count = jnp.int32(0)
    dead = jnp.int32(0)
    for j in range(n_q):
        top = sorted_q[j * per_q + per_q - 1]
        for i in range(n_k):
            live = sorted_k[i * per_k] <= top
            todo[count] = jnp.int32(j * n_k + i)
            count = count + live.astype(jnp.int32)
            dead = jnp.where(live, dead, j * n_k + i)
    for u in range(TOGETHER - 1):
        todo[count + u] = dead

    within = lax.broadcasted_iota(jnp.int32, (HALF, 128), 0)

    def one(t):
        j = todo[t] // n_k
        i = todo[t] % n_k
        q, g, k, v = qs[j], gs[j], ks[i], vs[i]
        posk = jnp.concatenate([within + sorted_k[i * per_k + b] * HALF for b in range(per_k)], axis=0)
        posk = jnp.concatenate([posk] * (HEADS * QT // 128), axis=1)
        s = dot_nt(k, q)
        p = jnp.where(posk <= posq_ref[j], jnp.exp2(s * (SCALE * LOG2E) - rows[j, 0:1, :]), 0.0)
        dp = dot_nt(v, g)
        ds = (p * (dp - rows[j, 1:2, :])).astype(jnp.bfloat16)
        dv[i] += dot(p.astype(jnp.bfloat16), g)
        dk[i] += dot(ds, q)
        dqt[j] += dot(kt[i], ds)

    def some(t, c):
        for u in range(TOGETHER):
            one(t * TOGETHER + u)
        return c

    lax.fori_loop(0, (count + TOGETHER - 1) // TOGETHER, some, 0)

    for j in range(n_q):
        for h in range(HEADS):
            back = dqt[j, :, h * QT:(h + 1) * QT].T
            half = back.astype(jnp.bfloat16)
            for b in range(per_q):
                to = order_q[j * per_q + b]
                cut = slice(b * HALF, (b + 1) * HALF)
                lane = slice(h * HD, (h + 1) * HD)
                dst = pl.multiple_of(to * HALF, HALF)
                far_ref[pl.ds(dst, HALF), lane] = half[cut]

                @pl.when(to < part_q)
                def _():
                    near_ref[pl.ds(dst, HALF), lane] = back[cut]
    for a in range(2):
        for b in range(part_k):
            place = rank_k[a * part_k + b]
            i = place // per_k
            r = pl.multiple_of(place % per_k * HALF, HALF)
            cut = slice(b * HALF, (b + 1) * HALF)
            out = own_ref if a == 0 else sib_ref
            out[cut, :HD] = dk[i, pl.ds(r, HALF), :].astype(out.dtype)
            out[cut, HD:] = dv[i, pl.ds(r, HALF), :].astype(out.dtype)


def tile_grads(q_parts, kv_parts, lists_q, lists_k):
    part = q_parts[0].shape[0] - STATS
    rows_q = 4 * part
    part_k = kv_parts[0].shape[0]
    rows_k = 2 * part_k
    n_q, n_k = rows_q // QT, rows_k // KT
    rank_q, order_q, sorted_q = lists_q
    rank_k, _, sorted_k = lists_k
    posq = positions(sorted_q).reshape(n_q, 1, QT)
    posq = jnp.concatenate([posq] * HEADS, axis=2)
    bf, f32 = jnp.bfloat16, jnp.float32
    return pl.pallas_call(
        tile_kernel,
        out_shape=(
            jax.ShapeDtypeStruct((part, HEADS * HD), f32),
            jax.ShapeDtypeStruct((rows_q, HEADS * HD), bf),
            jax.ShapeDtypeStruct((part_k, 2 * HD), f32),
            jax.ShapeDtypeStruct((part_k, 2 * HD), bf),
        ),
        in_specs=[SMEM] * 5 + [VMEM] * 7,
        out_specs=(VMEM,) * 4,
        scratch_shapes=[
            pltpu.VMEM((n_q, HEADS * QT, HD), bf),
            pltpu.VMEM((n_q, HEADS * QT, HD), bf),
            pltpu.VMEM((n_q + 4, STATS, HEADS * QT), f32),
            pltpu.VMEM((n_k, KT, HD), bf),
            pltpu.VMEM((n_k, KT, HD), bf),
            pltpu.VMEM((n_k, HD, KT), bf),
            pltpu.VMEM((n_q, HD, HEADS * QT), f32),
            pltpu.VMEM((n_k, KT, HD), f32),
            pltpu.VMEM((n_k, KT, HD), f32),
            pltpu.SMEM((n_q * n_k + TOGETHER,), jnp.int32),
        ],
        compiler_params=pltpu.CompilerParams(vmem_limit_bytes=40 * 1024 * 1024),
        cost_estimate=pl.CostEstimate(
            flops=rows_q * HEADS * rows_k * HD * 5,
            bytes_accessed=4 * 1024 * 1024,
            transcendentals=rows_q * HEADS * rows_k // 2,
        ),
    )(rank_q, order_q, sorted_q, rank_k, sorted_k, *q_parts, *kv_parts, posq)


def in_order(entries):
    n = entries.shape[0]
    rank = jnp.sum((entries[None, :] < entries[:, None]).astype(jnp.int32), axis=1)
    hit = rank[None, :] == jnp.arange(n, dtype=jnp.int32)[:, None]
    place = jnp.arange(n, dtype=jnp.int32)
    order = jnp.sum(jnp.where(hit, place[None, :], 0), axis=1)
    ordered = jnp.sum(jnp.where(hit, entries[None, :], 0), axis=1)
    return rank, order, ordered


def positions(ordered):
    return (ordered[:, None] * HALF + jnp.arange(HALF, dtype=jnp.int32)[None, :]).reshape(-1)


def pack_kv_kernel(k_ref, v_ref, out_ref):
    for n in range(out_ref.shape[0]):
        out_ref[n, :, :HD] = k_ref[...]
        out_ref[n, :, HD:] = v_ref[...]


def pack_kv(keys, values, copies):
    return pl.pallas_call(
        pack_kv_kernel,
        out_shape=jax.ShapeDtypeStruct((copies, keys.shape[0], 2 * HD), keys.dtype),
        in_specs=[VMEM] * 2,
        out_specs=VMEM,
    )(keys, values)


def pack_q_kernel(q_ref, g_ref, lse_ref, delta_ref, out_ref, wide):
    width = HEADS * HD
    rows = q_ref.shape[0]
    out_ref[:rows, :width] = q_ref[...]
    out_ref[:rows, width:] = g_ref[...]
    out_ref[rows:, :] = jnp.zeros((STATS, 2 * width), jnp.bfloat16)
    wide[...] = jnp.zeros_like(wide)
    n = 2 * HEADS
    for k in range(PIECES):
        wide[k * n:k * n + HEADS, :rows] = lse_ref[...]
        wide[k * n + HEADS:(k + 1) * n, :rows] = delta_ref[...]
    x = wide[...]
    piece = lax.broadcasted_iota(jnp.int32, x.shape, 0) // n
    out = jnp.zeros_like(x)
    for k in range(PIECES):
        part = x.astype(jnp.bfloat16).astype(jnp.float32)
        x = x - part
        out = jnp.where(piece == k, part, out)
    out_ref[rows:, :128] = out.astype(jnp.bfloat16)


def pack_q(queries, out_grad, log_sum, delta):
    rows = queries.shape[0]
    return pl.pallas_call(
        pack_q_kernel,
        out_shape=jax.ShapeDtypeStruct((rows + STATS, 2 * HEADS * HD), jnp.bfloat16),
        in_specs=[VMEM] * 4,
        out_specs=VMEM,
        scratch_shapes=[pltpu.VMEM((STATS, 128), jnp.float32)],
    )(queries, out_grad, log_sum.T, delta.T)


def join(parts):
    rows = parts[0].shape[0] - STATS
    stats = jnp.concatenate([p[rows:, :128] for p in parts], axis=1)
    return jnp.concatenate([p[:rows] for p in parts] + [stats], axis=0)


def from_offset(x, stage, d):
    pairs = []
    for ix in range(4):
        for iy in range(4):
            for core in range(2):
                tx, ty = ((ix + d) % 4, iy) if core == stage else (ix, (iy + d) % 4)
                pairs.append((place(ix, iy, core), place(tx, ty, core)))
    return lax.ppermute(x, ("x", "yl", "yh", "core"), pairs)


def place(ix, iy, core):
    return ((ix * 2 + iy % 2) * 2 + iy // 2) * 2 + core


def other_core(x):
    return lax.ppermute(x, "core", [(0, 1), (1, 0)])


def look_up(table, index):
    spot = jnp.arange(table.shape[0], dtype=jnp.int32)
    return jnp.sum(jnp.where(index[:, None] == spot[None, :], table[None, :], 0), axis=1)


def both_blocks(device):
    return (2 * device[:, None] + jnp.arange(2, dtype=jnp.int32)[None, :]).reshape(-1)


def local(queries, keys, values, out_grad, log_sum, delta, block_table):
    rows = queries.shape[0]
    width = HEADS * HD
    nx, nyl, nz, nyh, nc = (lax.axis_size(a) for a in ("x", "yl", "z", "yh", "core"))
    ix, iyl, iz, iyh, ic = (lax.axis_index(a) for a in ("x", "yl", "z", "yh", "core"))
    iy = iyh * nyl + iyl

    kv_own = lax.all_to_all(pack_kv(keys, values, nz), "z", split_axis=0, concat_axis=0, tiled=True)
    kv_own = kv_own.reshape(nz * rows, 2 * HD)

    def gather_q(turn, carried):
        packed = pack_q(queries, out_grad, log_sum, delta)
        line = join([packed] + [from_offset(packed, 0, d) for d in (1, 2, 3)])
        q_parts = [line] + [from_offset(line, 1, d) for d in (1, 2, 3)]
        table = block_table + jnp.minimum(turn, 0)
        spot = jnp.arange(16, dtype=jnp.int32)
        inner, outer = spot % 4, spot // 4
        x = (ix - jnp.where(ic == 0, inner, outer)) % nx
        y = (iy - jnp.where(ic == 0, outer, inner)) % (nyl * nyh)
        at = ((x * nyl + y % nyl) * nz + iz) * nyh * nc + y // nyl * nc + ic
        lists_q = in_order(look_up(table, both_blocks(at)))
        both = [((spot * nyh + iyh) * nc + c) * nx * nyl + ix * nyl + iyl for c in (ic, nc - 1 - ic)]
        lists_k = in_order(look_up(table, both_blocks(jnp.concatenate(both))))
        return q_parts, lists_q, lists_k

    empty = jax.tree.map(lambda x: jnp.zeros(x.shape, x.dtype), jax.eval_shape(lambda: gather_q(0, None)))
    turns = 1 + jnp.minimum(block_table[0], 0)
    q_parts, lists_q, lists_k = lax.fori_loop(0, turns, gather_q, empty)
    kv_own, q_parts = lax.optimization_barrier((kv_own, q_parts))
    kv_sib = other_core(kv_own)

    near, far, dkv_own, dkv_sib = tile_grads(q_parts, [kv_own, kv_sib], lists_q, lists_k)

    dkv = (dkv_own + other_core(dkv_sib).astype(jnp.float32)).astype(jnp.bfloat16)
    dkv = lax.all_to_all(dkv.reshape(nz, rows, 2 * HD), "z", split_axis=0, concat_axis=0, tiled=True)
    far = far.reshape(4, 4 * rows, width)
    for d in (1, 2, 3):
        near = near + from_offset(far[d], 1, 4 - d).astype(jnp.float32)
    near = near.reshape(4, rows, width)
    total = near[0]
    for d in (1, 2, 3):
        total = total + from_offset(near[d], 0, 4 - d)
    q_grad = (total * SCALE).astype(jnp.bfloat16)
    dkv = jnp.sum(dkv.astype(jnp.float32), axis=0)
    k_grad = (dkv[:, :HD] * SCALE).astype(jnp.bfloat16)
    v_grad = dkv[:, HD:].astype(jnp.bfloat16)
    return (q_grad, k_grad, v_grad)


def solution(mesh):
    fine = Mesh(mesh.devices.reshape(4, 2, 16, 2, 2), ("x", "yl", "z", "yh", "core"))
    q_rows = P(("x", "yl", "z", "yh", "core"), None)
    k_rows = P(("z", "yh", "core", "x", "yl"), None)
    return jax.shard_map(
        local,
        mesh=fine,
        in_specs=(q_rows, k_rows, k_rows, q_rows, q_rows, q_rows, P()),
        out_specs=(q_rows, k_rows, k_rows),
        check_vma=False,
    )
```

```python
import jax
import jax.numpy as jnp
from jax import lax
from jax.experimental import pallas as pl
from jax.experimental.pallas import tpu as pltpu
from jax.sharding import Mesh, PartitionSpec as P

HEADS = 2
HD = 128
HALF = 32
SCALE = HD ** (-0.5)
LOG2E = 1.4426950408889634
PIECES = 3
STATS = 16
QT = 256
KT = 256
TOGETHER = 2
VMEM = pl.BlockSpec(memory_space=pltpu.VMEM)
SMEM = pl.BlockSpec(memory_space=pltpu.SMEM)


def dot(a, b):
    return jnp.dot(a, b, preferred_element_type=jnp.float32)


def dot_nt(a, b):
    return lax.dot_general(a, b, (((1,), (1,)), ((), ())), preferred_element_type=jnp.float32)


def tile_kernel(rank_q, order_q, sorted_q, rank_k, sorted_k, *refs):
    q_refs = refs[:2]
    kv_ref, posq_ref, own_ref, sib_ref, dkv_ref = refs[2:7]
    qs, gs, stats, rows, ks, vs, kt, dqt, dqn, dk, dv, todo = refs[7:]
    n_q = qs.shape[0]
    n_k = ks.shape[0]
    per_q = QT // HALF
    per_k = KT // HALF
    lines = q_refs[0].shape[0]
    part_q = (q_refs[0].shape[1] - STATS) // HALF
    part_k = kv_ref.shape[0] // HALF

    for a in range(2):
        for n in range(lines):
            for b in range(part_q):
                place = rank_q[(a * lines + n) * part_q + b]
                j = place // per_q
                r = pl.multiple_of(place % per_q * HALF, HALF)
                cut = slice(b * HALF, (b + 1) * HALF)
                for h in range(HEADS):
                    qs[j, pl.ds(h * QT + r, HALF), :] = q_refs[a][n, cut, h * HD:(h + 1) * HD]
                    gs[j, pl.ds(h * QT + r, HALF), :] = q_refs[a][n, cut, (HEADS + h) * HD:(HEADS + h + 1) * HD]
            stats[a * lines + n] = q_refs[a][n, part_q * HALF:, :].astype(jnp.float32)
    for b in range(part_k):
        place = rank_k[b]
        i = place // per_k
        r = pl.multiple_of(place % per_k * HALF, HALF)
        cut = slice(b * HALF, (b + 1) * HALF)
        ks[i, pl.ds(r, HALF), :] = kv_ref[cut, :HD]
        vs[i, pl.ds(r, HALF), :] = kv_ref[cut, HD:]

    quarter = lax.broadcasted_iota(jnp.int32, (STATS, 128), 1) // HALF
    for t in range(n_q * QT // 128):
        line = jnp.zeros((STATS, 128), jnp.float32)
        for u in range(4):
            b = order_q[t * 4 + u]
            column = pl.multiple_of(b % part_q // 2 * 128, 128)
            piece = stats[b // part_q, :, pl.ds(column, 128)]
            piece = pltpu.roll(piece, (u - b % 2 + 4) % 4 * HALF, 1)
            line = jnp.where(quarter == u, piece, line)
        j, c = t // (QT // 128), t % (QT // 128)
        n = 2 * HEADS
        stat = line[:n] + line[n:2 * n] + line[2 * n:3 * n]
        for h in range(HEADS):
            cut = slice(h * QT + c * 128, h * QT + (c + 1) * 128)
            rows[j, 0:1, cut] = stat[h:h + 1] * LOG2E
            rows[j, 1:2, cut] = stat[HEADS + h:HEADS + h + 1]

    for i in range(n_k):
        kt[i] = ks[i].astype(jnp.float32).T.astype(jnp.bfloat16)

    dk[...] = jnp.zeros_like(dk)
    dv[...] = jnp.zeros_like(dv)
    dqt[...] = jnp.zeros_like(dqt)

    count = jnp.int32(0)
    dead = jnp.int32(0)
    for j in range(n_q):
        top = sorted_q[j * per_q + per_q - 1]
        for i in range(n_k):
            live = sorted_k[i * per_k] <= top
            todo[count] = jnp.int32(j * n_k + i)
            count = count + live.astype(jnp.int32)
            dead = jnp.where(live, dead, j * n_k + i)
    for u in range(TOGETHER - 1):
        todo[count + u] = dead

    within = lax.broadcasted_iota(jnp.int32, (HALF, 128), 0)

    def one(t):
        j = todo[t] // n_k
        i = todo[t] % n_k
        q, g, k, v = qs[j], gs[j], ks[i], vs[i]
        posk = jnp.concatenate([within + sorted_k[i * per_k + b] * HALF for b in range(per_k)], axis=0)
        posk = jnp.concatenate([posk] * (HEADS * QT // 128), axis=1)
        s = dot_nt(k, q)
        p = jnp.where(posk <= posq_ref[j], jnp.exp2(s * (SCALE * LOG2E) - rows[j, 0:1, :]), 0.0)
        dp = dot_nt(v, g)
        ds = (p * (dp - rows[j, 1:2, :])).astype(jnp.bfloat16)
        dv[i] += dot(p.astype(jnp.bfloat16), g)
        dk[i] += dot(ds, q)
        dqt[j] += dot(kt[i], ds)

    def some(t, c):
        for u in range(TOGETHER):
            one(t * TOGETHER + u)
        return c

    lax.fori_loop(0, (count + TOGETHER - 1) // TOGETHER, some, 0)

    for j in range(n_q):
        for h in range(HEADS):
            cut = slice(h * QT, (h + 1) * QT)
            dqn[j, cut, :] = dqt[j, :, cut].T
    for a, out in enumerate((own_ref, sib_ref)):
        for b in range(lines * part_q):
            place = rank_q[a * lines * part_q + b]
            j = place // per_q
            r = pl.multiple_of(place % per_q * HALF, HALF)
            cut = slice(b * HALF, (b + 1) * HALF)
            for h in range(HEADS):
                out[cut, h * HD:(h + 1) * HD] = dqn[j, pl.ds(h * QT + r, HALF), :]
    for b in range(part_k):
        place = rank_k[b]
        i = place // per_k
        r = pl.multiple_of(place % per_k * HALF, HALF)
        cut = slice(b * HALF, (b + 1) * HALF)
        dkv_ref[cut, :HD] = dk[i, pl.ds(r, HALF), :].astype(jnp.bfloat16)
        dkv_ref[cut, HD:] = dv[i, pl.ds(r, HALF), :].astype(jnp.bfloat16)


def tile_grads(q_parts, kv, lists_q, lists_k):
    lines, part = q_parts[0].shape[:2]
    rows_q = 2 * lines * (part - STATS)
    rows_k = kv.shape[0]
    n_q, n_k = rows_q // QT, rows_k // KT
    rank_q, order_q, sorted_q = lists_q
    rank_k, _, sorted_k = lists_k
    posq = positions(sorted_q).reshape(n_q, 1, QT)
    posq = jnp.concatenate([posq] * HEADS, axis=2)
    bf, f32 = jnp.bfloat16, jnp.float32
    return pl.pallas_call(
        tile_kernel,
        out_shape=(
            jax.ShapeDtypeStruct((rows_q // 2, HEADS * HD), f32),
            jax.ShapeDtypeStruct((rows_q // 2, HEADS * HD), f32),
            jax.ShapeDtypeStruct((rows_k, 2 * HD), bf),
        ),
        in_specs=[SMEM] * 5 + [VMEM] * 4,
        out_specs=(VMEM,) * 3,
        scratch_shapes=[
            pltpu.VMEM((n_q, HEADS * QT, HD), bf),
            pltpu.VMEM((n_q, HEADS * QT, HD), bf),
            pltpu.VMEM((2 * lines, STATS, 512), f32),
            pltpu.VMEM((n_q, 8, HEADS * QT), f32),
            pltpu.VMEM((n_k, KT, HD), bf),
            pltpu.VMEM((n_k, KT, HD), bf),
            pltpu.VMEM((n_k, HD, KT), bf),
            pltpu.VMEM((n_q, HD, HEADS * QT), f32),
            pltpu.VMEM((n_q, HEADS * QT, HD), f32),
            pltpu.VMEM((n_k, KT, HD), f32),
            pltpu.VMEM((n_k, KT, HD), f32),
            pltpu.SMEM((n_q * n_k + TOGETHER,), jnp.int32),
        ],
        compiler_params=pltpu.CompilerParams(vmem_limit_bytes=40 * 1024 * 1024),
        cost_estimate=pl.CostEstimate(
            flops=rows_q * HEADS * rows_k * HD * 5,
            bytes_accessed=4 * 1024 * 1024,
            transcendentals=rows_q * HEADS * rows_k // 2,
        ),
    )(rank_q, order_q, sorted_q, rank_k, sorted_k, *q_parts, kv, posq)


def in_order(entries):
    n = entries.shape[0]
    rank = jnp.sum((entries[None, :] < entries[:, None]).astype(jnp.int32), axis=1)
    hit = rank[None, :] == jnp.arange(n, dtype=jnp.int32)[:, None]
    place = jnp.arange(n, dtype=jnp.int32)
    order = jnp.sum(jnp.where(hit, place[None, :], 0), axis=1)
    ordered = jnp.sum(jnp.where(hit, entries[None, :], 0), axis=1)
    return rank, order, ordered


def positions(ordered):
    return (ordered[:, None] * HALF + jnp.arange(HALF, dtype=jnp.int32)[None, :]).reshape(-1)


def pack_kv_kernel(k_ref, v_ref, out_ref):
    for n in range(out_ref.shape[0]):
        out_ref[n, :, :HD] = k_ref[...]
        out_ref[n, :, HD:] = v_ref[...]


def pack_kv(keys, values, copies):
    return pl.pallas_call(
        pack_kv_kernel,
        out_shape=jax.ShapeDtypeStruct((copies, keys.shape[0], 2 * HD), keys.dtype),
        in_specs=[VMEM] * 2,
        out_specs=VMEM,
    )(keys, values)


def pack_q_kernel(q_ref, g_ref, lse_ref, delta_ref, out_ref, wide):
    width = HEADS * HD
    rows = q_ref.shape[0]
    out_ref[:rows, :width] = q_ref[...]
    out_ref[:rows, width:] = g_ref[...]
    out_ref[rows:, :] = jnp.zeros((STATS, 2 * width), jnp.bfloat16)
    wide[...] = jnp.zeros_like(wide)
    n = 2 * HEADS
    for k in range(PIECES):
        wide[k * n:k * n + HEADS, :rows] = lse_ref[...]
        wide[k * n + HEADS:(k + 1) * n, :rows] = delta_ref[...]
    x = wide[...]
    piece = lax.broadcasted_iota(jnp.int32, x.shape, 0) // n
    out = jnp.zeros_like(x)
    for k in range(PIECES):
        part = x.astype(jnp.bfloat16).astype(jnp.float32)
        x = x - part
        out = jnp.where(piece == k, part, out)
    out_ref[rows:, :128] = out.astype(jnp.bfloat16)


def pack_q(queries, out_grad, log_sum, delta):
    rows = queries.shape[0]
    return pl.pallas_call(
        pack_q_kernel,
        out_shape=jax.ShapeDtypeStruct((rows + STATS, 2 * HEADS * HD), jnp.bfloat16),
        in_specs=[VMEM] * 4,
        out_specs=VMEM,
        scratch_shapes=[pltpu.VMEM((STATS, 128), jnp.float32)],
    )(queries, out_grad, log_sum.T, delta.T)


def join(parts):
    rows = parts[0].shape[0] - STATS
    stats = jnp.concatenate([p[rows:, :128] for p in parts], axis=1)
    return jnp.concatenate([p[:rows] for p in parts] + [stats], axis=0)


def from_offset(x, stage, d):
    pairs = []
    for ix in range(4):
        for iy in range(4):
            for core in range(2):
                tx, ty = ((ix + d) % 4, iy) if core == stage else (ix, (iy + d) % 4)
                pairs.append((place(ix, iy, core), place(tx, ty, core)))
    return lax.ppermute(x, ("x", "yl", "yh", "core"), pairs)


def place(ix, iy, core):
    return ((ix * 2 + iy % 2) * 2 + iy // 2) * 2 + core


def other_core(x):
    return lax.ppermute(x, "core", [(0, 1), (1, 0)])


def look_up(table, index):
    spot = jnp.arange(table.shape[0], dtype=jnp.int32)
    return jnp.sum(jnp.where(index[:, None] == spot[None, :], table[None, :], 0), axis=1)


def both_blocks(device):
    return (2 * device[:, None] + jnp.arange(2, dtype=jnp.int32)[None, :]).reshape(-1)


def local(queries, keys, values, out_grad, log_sum, delta, block_table):
    rows = queries.shape[0]
    width = HEADS * HD
    nx, nyl, nz, nyh, nc = (lax.axis_size(a) for a in ("x", "yl", "z", "yh", "core"))
    ix, iyl, iz, iyh, ic = (lax.axis_index(a) for a in ("x", "yl", "z", "yh", "core"))
    iy = iyh * nyl + iyl

    kv = lax.all_to_all(pack_kv(keys, values, nz), "z", split_axis=0, concat_axis=0, tiled=True)
    kv = kv.reshape(nz * rows, 2 * HD)
    packed = pack_q(queries, out_grad, log_sum, delta)
    line = join([packed] + [from_offset(packed, 0, d) for d in (1, 2, 3)])
    q_own = jnp.stack([line] + [from_offset(line, 1, d) for d in (1, 2, 3)])
    table, q_own = lax.optimization_barrier((block_table, q_own))
    q_sib = other_core(q_own)

    spot = jnp.arange(nz, dtype=jnp.int32)
    lists_k = in_order(look_up(table, both_blocks(((spot * nyh + iyh) * nc + ic) * nx * nyl + ix * nyl + iyl)))
    at = []
    for c in (ic, nc - 1 - ic):
        along_x, along_y = jnp.where(c == 0, spot % 4, spot // 4), jnp.where(c == 0, spot // 4, spot % 4)
        x, y = (ix - along_x) % nx, (iy - along_y) % (nyl * nyh)
        at.append(((x * nyl + y % nyl) * nz + iz) * nyh * nc + y // nyl * nc + c)
    lists_q = in_order(look_up(table, both_blocks(jnp.concatenate(at))))

    dq, dq_sib, dkv = tile_grads([q_own, q_sib], kv, lists_q, lists_k)

    dkv = lax.all_to_all(dkv.reshape(nz, rows, 2 * HD), "z", split_axis=0, concat_axis=0, tiled=True)
    dq = dq + other_core(dq_sib)
    near, far = dq[:4 * rows], dq.astype(jnp.bfloat16)
    far = far.reshape(4, 4 * rows, width)
    for d in (1, 2, 3):
        near = near + from_offset(far[d], 1, 4 - d).astype(jnp.float32)
    near = near.reshape(4, rows, width)
    total = near[0]
    for d in (1, 2, 3):
        total = total + from_offset(near[d], 0, 4 - d)
    q_grad = (total * SCALE).astype(jnp.bfloat16)
    dkv = jnp.sum(dkv.astype(jnp.float32), axis=0)
    k_grad = (dkv[:, :HD] * SCALE).astype(jnp.bfloat16)
    v_grad = dkv[:, HD:].astype(jnp.bfloat16)
    return (q_grad, k_grad, v_grad)


def solution(mesh):
    fine = Mesh(mesh.devices.reshape(4, 2, 16, 2, 2), ("x", "yl", "z", "yh", "core"))
    q_rows = P(("x", "yl", "z", "yh", "core"), None)
    k_rows = P(("z", "yh", "core", "x", "yl"), None)
    return jax.shard_map(
        local,
        mesh=fine,
        in_specs=(q_rows, k_rows, k_rows, q_rows, q_rows, q_rows, P()),
        out_specs=(q_rows, k_rows, k_rows),
        check_vma=False,
    )
```

```python
import jax
import jax.numpy as jnp
from jax import lax
from jax.experimental import pallas as pl
from jax.experimental.pallas import tpu as pltpu
from jax.sharding import Mesh, PartitionSpec as P

HEADS = 2
HD = 128
HALF = 32
SCALE = HD ** (-0.5)
LOG2E = 1.4426950408889634
PIECES = 3
STATS = 16
QT = 256
KT = 256
TOGETHER = 4
VMEM = pl.BlockSpec(memory_space=pltpu.VMEM)
SMEM = pl.BlockSpec(memory_space=pltpu.SMEM)


def dot(a, b):
    return jnp.dot(a, b, preferred_element_type=jnp.float32)


def dot_nt(a, b):
    return lax.dot_general(a, b, (((1,), (1,)), ((), ())), preferred_element_type=jnp.float32)


def tile_kernel(rank_q, order_q, sorted_q, rank_k, sorted_k, *refs):
    q_refs = refs[:2]
    kv_ref, posq_ref, own_ref, sib_ref, dkv_ref = refs[2:7]
    qs, gs, stats, rows, ks, vs, kt, dqt, dqn, dk, dv, todo = refs[7:]
    n_q = qs.shape[0]
    n_k = ks.shape[0]
    per_q = QT // HALF
    per_k = KT // HALF
    lines = q_refs[0].shape[0]
    part_q = (q_refs[0].shape[1] - STATS) // HALF
    part_k = kv_ref.shape[0] // HALF

    for a in range(2):
        for n in range(lines):
            for b in range(part_q):
                place = rank_q[(a * lines + n) * part_q + b]
                j = place // per_q
                r = pl.multiple_of(place % per_q * HALF, HALF)
                cut = slice(b * HALF, (b + 1) * HALF)
                for h in range(HEADS):
                    qs[j, pl.ds(h * QT + r, HALF), :] = q_refs[a][n, cut, h * HD:(h + 1) * HD]
                    gs[j, pl.ds(h * QT + r, HALF), :] = q_refs[a][n, cut, (HEADS + h) * HD:(HEADS + h + 1) * HD]
            stats[a * lines + n] = q_refs[a][n, part_q * HALF:, :].astype(jnp.float32)
    for b in range(part_k):
        place = rank_k[b]
        i = place // per_k
        r = pl.multiple_of(place % per_k * HALF, HALF)
        cut = slice(b * HALF, (b + 1) * HALF)
        ks[i, pl.ds(r, HALF), :] = kv_ref[cut, :HD]
        vs[i, pl.ds(r, HALF), :] = kv_ref[cut, HD:]

    quarter = lax.broadcasted_iota(jnp.int32, (STATS, 128), 1) // HALF
    for t in range(n_q * QT // 128):
        line = jnp.zeros((STATS, 128), jnp.float32)
        for u in range(4):
            b = order_q[t * 4 + u]
            column = pl.multiple_of(b % part_q // 2 * 128, 128)
            piece = stats[b // part_q, :, pl.ds(column, 128)]
            piece = pltpu.roll(piece, (u - b % 2 + 4) % 4 * HALF, 1)
            line = jnp.where(quarter == u, piece, line)
        j, c = t // (QT // 128), t % (QT // 128)
        n = 2 * HEADS
        stat = line[:n] + line[n:2 * n] + line[2 * n:3 * n]
        for h in range(HEADS):
            cut = slice(h * QT + c * 128, h * QT + (c + 1) * 128)
            rows[j, 0:1, cut] = stat[h:h + 1] * LOG2E
            rows[j, 1:2, cut] = stat[HEADS + h:HEADS + h + 1]

    for i in range(n_k):
        kt[i] = ks[i].astype(jnp.float32).T.astype(jnp.bfloat16)

    dk[...] = jnp.zeros_like(dk)
    dv[...] = jnp.zeros_like(dv)
    dqt[...] = jnp.zeros_like(dqt)

    count = jnp.int32(0)
    dead = jnp.int32(0)
    for j in range(n_q):
        top = sorted_q[j * per_q + per_q - 1]
        for i in range(n_k):
            live = sorted_k[i * per_k] <= top
            todo[count] = jnp.int32(j * n_k + i)
            count = count + live.astype(jnp.int32)
            dead = jnp.where(live, dead, j * n_k + i)
    for u in range(TOGETHER - 1):
        todo[count + u] = dead

    within = lax.broadcasted_iota(jnp.int32, (HALF, 128), 0)

    def one(t):
        j = todo[t] // n_k
        i = todo[t] % n_k
        q, g, k, v = qs[j], gs[j], ks[i], vs[i]
        posk = jnp.concatenate([within + sorted_k[i * per_k + b] * HALF for b in range(per_k)], axis=0)
        posk = jnp.concatenate([posk] * (HEADS * QT // 128), axis=1)
        s = dot_nt(k, q)
        p = jnp.where(posk <= posq_ref[j], jnp.exp2(s * (SCALE * LOG2E) - rows[j, 0:1, :]), 0.0)
        dp = dot_nt(v, g)
        ds = (p * (dp - rows[j, 1:2, :])).astype(jnp.bfloat16)
        dv[i] += dot(p.astype(jnp.bfloat16), g)
        dk[i] += dot(ds, q)
        dqt[j] += dot(kt[i], ds)

    def some(t, c):
        for u in range(TOGETHER):
            one(t * TOGETHER + u)
        return c

    lax.fori_loop(0, (count + TOGETHER - 1) // TOGETHER, some, 0)

    for j in range(n_q):
        for h in range(HEADS):
            cut = slice(h * QT, (h + 1) * QT)
            dqn[j, cut, :] = dqt[j, :, cut].T
    for a, out in enumerate((own_ref, sib_ref)):
        for b in range(lines * part_q):
            place = rank_q[a * lines * part_q + b]
            j = place // per_q
            r = pl.multiple_of(place % per_q * HALF, HALF)
            cut = slice(b * HALF, (b + 1) * HALF)
            for h in range(HEADS):
                out[cut, h * HD:(h + 1) * HD] = dqn[j, pl.ds(h * QT + r, HALF), :]
    for b in range(part_k):
        place = rank_k[b]
        i = place // per_k
        r = pl.multiple_of(place % per_k * HALF, HALF)
        cut = slice(b * HALF, (b + 1) * HALF)
        dkv_ref[cut, :HD] = dk[i, pl.ds(r, HALF), :].astype(jnp.bfloat16)
        dkv_ref[cut, HD:] = dv[i, pl.ds(r, HALF), :].astype(jnp.bfloat16)


def tile_grads(q_parts, kv, lists_q, lists_k):
    lines, part = q_parts[0].shape[:2]
    rows_q = 2 * lines * (part - STATS)
    rows_k = kv.shape[0]
    n_q, n_k = rows_q // QT, rows_k // KT
    rank_q, order_q, sorted_q = lists_q
    rank_k, _, sorted_k = lists_k
    posq = positions(sorted_q).reshape(n_q, 1, QT)
    posq = jnp.concatenate([posq] * HEADS, axis=2)
    bf, f32 = jnp.bfloat16, jnp.float32
    return pl.pallas_call(
        tile_kernel,
        out_shape=(
            jax.ShapeDtypeStruct((rows_q // 2, HEADS * HD), f32),
            jax.ShapeDtypeStruct((rows_q // 2, HEADS * HD), f32),
            jax.ShapeDtypeStruct((rows_k, 2 * HD), bf),
        ),
        in_specs=[SMEM] * 5 + [VMEM] * 4,
        out_specs=(VMEM,) * 3,
        scratch_shapes=[
            pltpu.VMEM((n_q, HEADS * QT, HD), bf),
            pltpu.VMEM((n_q, HEADS * QT, HD), bf),
            pltpu.VMEM((2 * lines, STATS, 512), f32),
            pltpu.VMEM((n_q, 8, HEADS * QT), f32),
            pltpu.VMEM((n_k, KT, HD), bf),
            pltpu.VMEM((n_k, KT, HD), bf),
            pltpu.VMEM((n_k, HD, KT), bf),
            pltpu.VMEM((n_q, HD, HEADS * QT), f32),
            pltpu.VMEM((n_q, HEADS * QT, HD), f32),
            pltpu.VMEM((n_k, KT, HD), f32),
            pltpu.VMEM((n_k, KT, HD), f32),
            pltpu.SMEM((n_q * n_k + TOGETHER,), jnp.int32),
        ],
        compiler_params=pltpu.CompilerParams(vmem_limit_bytes=40 * 1024 * 1024),
        cost_estimate=pl.CostEstimate(
            flops=rows_q * HEADS * rows_k * HD * 5,
            bytes_accessed=4 * 1024 * 1024,
            transcendentals=rows_q * HEADS * rows_k // 2,
        ),
    )(rank_q, order_q, sorted_q, rank_k, sorted_k, *q_parts, kv, posq)


def in_order(entries):
    n = entries.shape[0]
    rank = jnp.sum((entries[None, :] < entries[:, None]).astype(jnp.int32), axis=1)
    hit = rank[None, :] == jnp.arange(n, dtype=jnp.int32)[:, None]
    place = jnp.arange(n, dtype=jnp.int32)
    order = jnp.sum(jnp.where(hit, place[None, :], 0), axis=1)
    ordered = jnp.sum(jnp.where(hit, entries[None, :], 0), axis=1)
    return rank, order, ordered


def positions(ordered):
    return (ordered[:, None] * HALF + jnp.arange(HALF, dtype=jnp.int32)[None, :]).reshape(-1)


def pack_q_kernel(q_ref, g_ref, lse_ref, delta_ref, out_ref, wide):
    width = HEADS * HD
    rows = q_ref.shape[0]
    out_ref[:rows, :width] = q_ref[...]
    out_ref[:rows, width:] = g_ref[...]
    out_ref[rows:, :] = jnp.zeros((STATS, 2 * width), jnp.bfloat16)
    wide[...] = jnp.zeros_like(wide)
    n = 2 * HEADS
    for k in range(PIECES):
        wide[k * n:k * n + HEADS, :rows] = lse_ref[...]
        wide[k * n + HEADS:(k + 1) * n, :rows] = delta_ref[...]
    x = wide[...]
    piece = lax.broadcasted_iota(jnp.int32, x.shape, 0) // n
    out = jnp.zeros_like(x)
    for k in range(PIECES):
        part = x.astype(jnp.bfloat16).astype(jnp.float32)
        x = x - part
        out = jnp.where(piece == k, part, out)
    out_ref[rows:, :128] = out.astype(jnp.bfloat16)


def pack_q(queries, out_grad, log_sum, delta):
    rows = queries.shape[0]
    return pl.pallas_call(
        pack_q_kernel,
        out_shape=jax.ShapeDtypeStruct((rows + STATS, 2 * HEADS * HD), jnp.bfloat16),
        in_specs=[VMEM] * 4,
        out_specs=VMEM,
        scratch_shapes=[pltpu.VMEM((STATS, 128), jnp.float32)],
    )(queries, out_grad, log_sum.T, delta.T)


def join(parts):
    rows = parts[0].shape[0] - STATS
    stats = jnp.concatenate([p[rows:, :128] for p in parts], axis=1)
    return jnp.concatenate([p[:rows] for p in parts] + [stats], axis=0)


def from_offset(x, stage, d):
    pairs = []
    for ix in range(4):
        for iy in range(4):
            for core in range(2):
                tx, ty = ((ix + d) % 4, iy) if core == stage else (ix, (iy + d) % 4)
                pairs.append((place(ix, iy, core), place(tx, ty, core)))
    return lax.ppermute(x, ("x", "yl", "yh", "core"), pairs)


def place(ix, iy, core):
    return ((ix * 2 + iy % 2) * 2 + iy // 2) * 2 + core


def other_core(x):
    return lax.ppermute(x, "core", [(0, 1), (1, 0)])


def look_up(table, index):
    spot = jnp.arange(table.shape[0], dtype=jnp.int32)
    return jnp.sum(jnp.where(index[:, None] == spot[None, :], table[None, :], 0), axis=1)


def both_blocks(device):
    return (2 * device[:, None] + jnp.arange(2, dtype=jnp.int32)[None, :]).reshape(-1)


def local(queries, keys, values, out_grad, log_sum, delta, block_table):
    rows = queries.shape[0]
    width = HEADS * HD
    nx, nyl, nz, nyh, nc = (lax.axis_size(a) for a in ("x", "yl", "z", "yh", "core"))
    ix, iyl, iz, iyh, ic = (lax.axis_index(a) for a in ("x", "yl", "z", "yh", "core"))
    iy = iyh * nyl + iyl

    kv = jnp.concatenate([keys, values], axis=1)
    kv = lax.all_to_all(jnp.broadcast_to(kv[None], (nz,) + kv.shape), "z", split_axis=0, concat_axis=0, tiled=True)
    kv = kv.reshape(nz * rows, 2 * HD)
    packed = pack_q(queries, out_grad, log_sum, delta)
    line = join([packed] + [from_offset(packed, 0, d) for d in (1, 2, 3)])
    q_own = jnp.stack([line] + [from_offset(line, 1, d) for d in (1, 2, 3)])
    table, q_own, kv = lax.optimization_barrier((block_table, q_own, kv))
    q_sib = other_core(q_own)

    spot = jnp.arange(nz, dtype=jnp.int32)
    lists_k = in_order(look_up(table, both_blocks(((spot * nyh + iyh) * nc + ic) * nx * nyl + ix * nyl + iyl)))
    at = []
    for c in (ic, nc - 1 - ic):
        along_x, along_y = jnp.where(c == 0, spot % 4, spot // 4), jnp.where(c == 0, spot // 4, spot % 4)
        x, y = (ix - along_x) % nx, (iy - along_y) % (nyl * nyh)
        at.append(((x * nyl + y % nyl) * nz + iz) * nyh * nc + y // nyl * nc + c)
    lists_q = in_order(look_up(table, both_blocks(jnp.concatenate(at))))

    dq, dq_sib, dkv = tile_grads([q_own, q_sib], kv, lists_q, lists_k)

    dkv = lax.all_to_all(dkv.reshape(nz, rows, 2 * HD), "z", split_axis=0, concat_axis=0, tiled=True)
    dq = dq + other_core(dq_sib)
    near, far = dq[:4 * rows], dq.astype(jnp.bfloat16)
    far = far.reshape(4, 4 * rows, width)
    for d in (1, 2, 3):
        near = near + from_offset(far[d], 1, 4 - d).astype(jnp.float32)
    near = near.reshape(4, rows, width)
    total = near[0]
    for d in (1, 2, 3):
        total = total + from_offset(near[d], 0, 4 - d)
    q_grad = (total * SCALE).astype(jnp.bfloat16)
    dkv = jnp.sum(dkv.astype(jnp.float32), axis=0)
    k_grad = (dkv[:, :HD] * SCALE).astype(jnp.bfloat16)
    v_grad = dkv[:, HD:].astype(jnp.bfloat16)
    return (q_grad, k_grad, v_grad)


def solution(mesh):
    fine = Mesh(mesh.devices.reshape(4, 2, 16, 2, 2), ("x", "yl", "z", "yh", "core"))
    q_rows = P(("x", "yl", "z", "yh", "core"), None)
    k_rows = P(("z", "yh", "core", "x", "yl"), None)
    return jax.shard_map(
        local,
        mesh=fine,
        in_specs=(q_rows, k_rows, k_rows, q_rows, q_rows, q_rows, P()),
        out_specs=(q_rows, k_rows, k_rows),
        check_vma=False,
    )
```

```python
import jax
import jax.numpy as jnp
from jax import lax
from jax.experimental import pallas as pl
from jax.experimental.pallas import tpu as pltpu
from jax.sharding import Mesh, PartitionSpec as P

HEADS = 2
HD = 128
HALF = 32
SCALE = HD ** (-0.5)
LOG2E = 1.4426950408889634
PIECES = 3
STATS = 16
QT = 256
KT = 256
VMEM = pl.BlockSpec(memory_space=pltpu.VMEM)
SMEM = pl.BlockSpec(memory_space=pltpu.SMEM)


def dot(a, b):
    return jnp.dot(a, b, preferred_element_type=jnp.float32)


def dot_nt(a, b):
    return lax.dot_general(a, b, (((1,), (1,)), ((), ())), preferred_element_type=jnp.float32)


def tile_kernel(rank_q, order_q, sorted_q, rank_k, sorted_k, *refs):
    q_refs = refs[:2]
    kv_ref, posq_ref, own_ref, sib_ref, dkv_ref = refs[2:7]
    qs, gs, stats, rows, ks, vs, kt, dqt, dqn, dk, dv, todo = refs[7:]
    n_q = qs.shape[0]
    n_k = ks.shape[0]
    per_q = QT // HALF
    per_k = KT // HALF
    lines = q_refs[0].shape[0]
    part_q = (q_refs[0].shape[1] - STATS) // HALF
    part_k = kv_ref.shape[0] // HALF

    for a in range(2):
        for n in range(lines):
            for b in range(part_q):
                place = rank_q[(a * lines + n) * part_q + b]
                j = place // per_q
                r = pl.multiple_of(place % per_q * HALF, HALF)
                cut = slice(b * HALF, (b + 1) * HALF)
                for h in range(HEADS):
                    qs[j, pl.ds(h * QT + r, HALF), :] = q_refs[a][n, cut, h * HD:(h + 1) * HD]
                    gs[j, pl.ds(h * QT + r, HALF), :] = q_refs[a][n, cut, (HEADS + h) * HD:(HEADS + h + 1) * HD]
            stats[a * lines + n] = q_refs[a][n, part_q * HALF:, :].astype(jnp.float32)
    for b in range(part_k):
        place = rank_k[b]
        i = place // per_k
        r = pl.multiple_of(place % per_k * HALF, HALF)
        cut = slice(b * HALF, (b + 1) * HALF)
        ks[i, pl.ds(r, HALF), :] = kv_ref[cut, :HD]
        vs[i, pl.ds(r, HALF), :] = kv_ref[cut, HD:]

    quarter = lax.broadcasted_iota(jnp.int32, (STATS, 128), 1) // HALF
    for t in range(n_q * QT // 128):
        line = jnp.zeros((STATS, 128), jnp.float32)
        for u in range(4):
            b = order_q[t * 4 + u]
            column = pl.multiple_of(b % part_q // 2 * 128, 128)
            piece = stats[b // part_q, :, pl.ds(column, 128)]
            piece = pltpu.roll(piece, (u - b % 2 + 4) % 4 * HALF, 1)
            line = jnp.where(quarter == u, piece, line)
        j, c = t // (QT // 128), t % (QT // 128)
        n = 2 * HEADS
        stat = line[:n] + line[n:2 * n] + line[2 * n:3 * n]
        for h in range(HEADS):
            cut = slice(h * QT + c * 128, h * QT + (c + 1) * 128)
            rows[j, 0:1, cut] = stat[h:h + 1] * LOG2E
            rows[j, 1:2, cut] = stat[HEADS + h:HEADS + h + 1]

    for i in range(n_k):
        kt[i] = ks[i].astype(jnp.float32).T.astype(jnp.bfloat16)

    dk[...] = jnp.zeros_like(dk)
    dv[...] = jnp.zeros_like(dv)
    dqt[...] = jnp.zeros_like(dqt)

    count = jnp.int32(0)
    dead = jnp.int32(0)
    for j in range(n_q):
        top = sorted_q[j * per_q + per_q - 1]
        for i in range(n_k):
            live = sorted_k[i * per_k] <= top
            todo[count] = jnp.int32(j * n_k + i)
            count = count + live.astype(jnp.int32)
            dead = jnp.where(live, dead, j * n_k + i)
    todo[count] = dead

    within = lax.broadcasted_iota(jnp.int32, (HALF, 128), 0)

    def one(t):
        j = todo[t] // n_k
        i = todo[t] % n_k
        q, g, k, v = qs[j], gs[j], ks[i], vs[i]
        posk = jnp.concatenate([within + sorted_k[i * per_k + b] * HALF for b in range(per_k)], axis=0)
        posk = jnp.concatenate([posk] * (HEADS * QT // 128), axis=1)
        s = dot_nt(k, q)
        p = jnp.where(posk <= posq_ref[j], jnp.exp2(s * (SCALE * LOG2E) - rows[j, 0:1, :]), 0.0)
        dp = dot_nt(v, g)
        ds = (p * (dp - rows[j, 1:2, :])).astype(jnp.bfloat16)
        dv[i] += dot(p.astype(jnp.bfloat16), g)
        dk[i] += dot(ds, q)
        dqt[j] += dot(kt[i], ds)

    def four(t, c):
        for u in range(4):
            one(t * 4 + u)
        return c

    def two(t, c):
        for u in range(2):
            one(t * 2 + u)
        return c

    lax.fori_loop(0, count // 4, four, 0)
    lax.fori_loop(count // 4 * 2, (count + 1) // 2, two, 0)

    for j in range(n_q):
        for h in range(HEADS):
            cut = slice(h * QT, (h + 1) * QT)
            dqn[j, cut, :] = dqt[j, :, cut].T
    for a, out in enumerate((own_ref, sib_ref)):
        for b in range(lines * part_q):
            place = rank_q[a * lines * part_q + b]
            j = place // per_q
            r = pl.multiple_of(place % per_q * HALF, HALF)
            cut = slice(b * HALF, (b + 1) * HALF)
            for h in range(HEADS):
                out[cut, h * HD:(h + 1) * HD] = dqn[j, pl.ds(h * QT + r, HALF), :]
    for b in range(part_k):
        place = rank_k[b]
        i = place // per_k
        r = pl.multiple_of(place % per_k * HALF, HALF)
        cut = slice(b * HALF, (b + 1) * HALF)
        dkv_ref[cut, :HD] = dk[i, pl.ds(r, HALF), :].astype(jnp.bfloat16)
        dkv_ref[cut, HD:] = dv[i, pl.ds(r, HALF), :].astype(jnp.bfloat16)


def tile_grads(q_parts, kv, lists_q, lists_k):
    lines, part = q_parts[0].shape[:2]
    rows_q = 2 * lines * (part - STATS)
    rows_k = kv.shape[0]
    n_q, n_k = rows_q // QT, rows_k // KT
    rank_q, order_q, sorted_q = lists_q
    rank_k, _, sorted_k = lists_k
    posq = positions(sorted_q).reshape(n_q, 1, QT)
    posq = jnp.concatenate([posq] * HEADS, axis=2)
    bf, f32 = jnp.bfloat16, jnp.float32
    return pl.pallas_call(
        tile_kernel,
        out_shape=(
            jax.ShapeDtypeStruct((rows_q // 2, HEADS * HD), f32),
            jax.ShapeDtypeStruct((rows_q // 2, HEADS * HD), f32),
            jax.ShapeDtypeStruct((rows_k, 2 * HD), bf),
        ),
        in_specs=[SMEM] * 5 + [VMEM] * 4,
        out_specs=(VMEM,) * 3,
        scratch_shapes=[
            pltpu.VMEM((n_q, HEADS * QT, HD), bf),
            pltpu.VMEM((n_q, HEADS * QT, HD), bf),
            pltpu.VMEM((2 * lines, STATS, 512), f32),
            pltpu.VMEM((n_q, 8, HEADS * QT), f32),
            pltpu.VMEM((n_k, KT, HD), bf),
            pltpu.VMEM((n_k, KT, HD), bf),
            pltpu.VMEM((n_k, HD, KT), bf),
            pltpu.VMEM((n_q, HD, HEADS * QT), f32),
            pltpu.VMEM((n_q, HEADS * QT, HD), f32),
            pltpu.VMEM((n_k, KT, HD), f32),
            pltpu.VMEM((n_k, KT, HD), f32),
            pltpu.SMEM((n_q * n_k + 1,), jnp.int32),
        ],
        compiler_params=pltpu.CompilerParams(vmem_limit_bytes=40 * 1024 * 1024),
        cost_estimate=pl.CostEstimate(
            flops=rows_q * HEADS * rows_k * HD * 5,
            bytes_accessed=4 * 1024 * 1024,
            transcendentals=rows_q * HEADS * rows_k // 2,
        ),
    )(rank_q, order_q, sorted_q, rank_k, sorted_k, *q_parts, kv, posq)


def in_order(entries):
    n = entries.shape[0]
    rank = jnp.sum((entries[None, :] < entries[:, None]).astype(jnp.int32), axis=1)
    hit = rank[None, :] == jnp.arange(n, dtype=jnp.int32)[:, None]
    place = jnp.arange(n, dtype=jnp.int32)
    order = jnp.sum(jnp.where(hit, place[None, :], 0), axis=1)
    ordered = jnp.sum(jnp.where(hit, entries[None, :], 0), axis=1)
    return rank, order, ordered


def positions(ordered):
    return (ordered[:, None] * HALF + jnp.arange(HALF, dtype=jnp.int32)[None, :]).reshape(-1)


def pack_q_kernel(q_ref, g_ref, lse_ref, delta_ref, out_ref, wide):
    width = HEADS * HD
    rows = q_ref.shape[0]
    out_ref[:rows, :width] = q_ref[...]
    out_ref[:rows, width:] = g_ref[...]
    out_ref[rows:, :] = jnp.zeros((STATS, 2 * width), jnp.bfloat16)
    wide[...] = jnp.zeros_like(wide)
    n = 2 * HEADS
    for k in range(PIECES):
        wide[k * n:k * n + HEADS, :rows] = lse_ref[...]
        wide[k * n + HEADS:(k + 1) * n, :rows] = delta_ref[...]
    x = wide[...]
    piece = lax.broadcasted_iota(jnp.int32, x.shape, 0) // n
    out = jnp.zeros_like(x)
    for k in range(PIECES):
        part = x.astype(jnp.bfloat16).astype(jnp.float32)
        x = x - part
        out = jnp.where(piece == k, part, out)
    out_ref[rows:, :128] = out.astype(jnp.bfloat16)


def pack_q(queries, out_grad, log_sum, delta):
    rows = queries.shape[0]
    return pl.pallas_call(
        pack_q_kernel,
        out_shape=jax.ShapeDtypeStruct((rows + STATS, 2 * HEADS * HD), jnp.bfloat16),
        in_specs=[VMEM] * 4,
        out_specs=VMEM,
        scratch_shapes=[pltpu.VMEM((STATS, 128), jnp.float32)],
    )(queries, out_grad, log_sum.T, delta.T)


def join(parts):
    rows = parts[0].shape[0] - STATS
    stats = jnp.concatenate([p[rows:, :128] for p in parts], axis=1)
    return jnp.concatenate([p[:rows] for p in parts] + [stats], axis=0)


def from_offset(x, stage, d):
    pairs = []
    for ix in range(4):
        for iy in range(4):
            for core in range(2):
                tx, ty = ((ix + d) % 4, iy) if core == stage else (ix, (iy + d) % 4)
                pairs.append((place(ix, iy, core), place(tx, ty, core)))
    return lax.ppermute(x, ("x", "yl", "yh", "core"), pairs)


def place(ix, iy, core):
    return ((ix * 2 + iy % 2) * 2 + iy // 2) * 2 + core


def other_core(x):
    return lax.ppermute(x, "core", [(0, 1), (1, 0)])


def look_up(table, index):
    spot = jnp.arange(table.shape[0], dtype=jnp.int32)
    return jnp.sum(jnp.where(index[:, None] == spot[None, :], table[None, :], 0), axis=1)


def both_blocks(device):
    return (2 * device[:, None] + jnp.arange(2, dtype=jnp.int32)[None, :]).reshape(-1)


def local(queries, keys, values, out_grad, log_sum, delta, block_table):
    rows = queries.shape[0]
    width = HEADS * HD
    nx, nyl, nz, nyh, nc = (lax.axis_size(a) for a in ("x", "yl", "z", "yh", "core"))
    ix, iyl, iz, iyh, ic = (lax.axis_index(a) for a in ("x", "yl", "z", "yh", "core"))
    iy = iyh * nyl + iyl

    kv = jnp.concatenate([keys, values], axis=1)
    kv = lax.all_to_all(jnp.broadcast_to(kv[None], (nz,) + kv.shape), "z", split_axis=0, concat_axis=0, tiled=True)
    kv = kv.reshape(nz * rows, 2 * HD)
    packed = pack_q(queries, out_grad, log_sum, delta)
    line = join([packed] + [from_offset(packed, 0, d) for d in (1, 2, 3)])
    q_own = jnp.stack([line] + [from_offset(line, 1, d) for d in (1, 2, 3)])
    table, q_own = lax.optimization_barrier((block_table, q_own))
    q_sib = other_core(q_own)

    spot = jnp.arange(nz, dtype=jnp.int32)
    lists_k = in_order(look_up(table, both_blocks(((spot * nyh + iyh) * nc + ic) * nx * nyl + ix * nyl + iyl)))
    at = []
    for c in (ic, nc - 1 - ic):
        along_x, along_y = jnp.where(c == 0, spot % 4, spot // 4), jnp.where(c == 0, spot // 4, spot % 4)
        x, y = (ix - along_x) % nx, (iy - along_y) % (nyl * nyh)
        at.append(((x * nyl + y % nyl) * nz + iz) * nyh * nc + y // nyl * nc + c)
    lists_q = in_order(look_up(table, both_blocks(jnp.concatenate(at))))

    dq, dq_sib, dkv = tile_grads([q_own, q_sib], kv, lists_q, lists_k)

    dkv = lax.all_to_all(dkv.reshape(nz, rows, 2 * HD), "z", split_axis=0, concat_axis=0, tiled=True)
    dq = dq + other_core(dq_sib)
    near, far = dq[:4 * rows], dq.astype(jnp.bfloat16)
    far = far.reshape(4, 4 * rows, width)
    for d in (1, 2, 3):
        near = near + from_offset(far[d], 1, 4 - d).astype(jnp.float32)
    near = near.reshape(4, rows, width)
    total = near[0]
    for d in (1, 2, 3):
        total = total + from_offset(near[d], 0, 4 - d)
    q_grad = (total * SCALE).astype(jnp.bfloat16)
    dkv = jnp.sum(dkv.astype(jnp.float32), axis=0)
    k_grad = (dkv[:, :HD] * SCALE).astype(jnp.bfloat16)
    v_grad = dkv[:, HD:].astype(jnp.bfloat16)
    return (q_grad, k_grad, v_grad)


def solution(mesh):
    fine = Mesh(mesh.devices.reshape(4, 2, 16, 2, 2), ("x", "yl", "z", "yh", "core"))
    q_rows = P(("x", "yl", "z", "yh", "core"), None)
    k_rows = P(("z", "yh", "core", "x", "yl"), None)
    return jax.shard_map(
        local,
        mesh=fine,
        in_specs=(q_rows, k_rows, k_rows, q_rows, q_rows, q_rows, P()),
        out_specs=(q_rows, k_rows, k_rows),
        check_vma=False,
    )
```

```python
import jax
import jax.numpy as jnp
from jax import lax
from jax.experimental import pallas as pl
from jax.experimental.pallas import tpu as pltpu
from jax.sharding import Mesh, PartitionSpec as P

HEADS = 2
HD = 128
HALF = 32
SCALE = HD ** (-0.5)
LOG2E = 1.4426950408889634
PIECES = 3
STATS = 16
QT = 256
KT = 256
VMEM = pl.BlockSpec(memory_space=pltpu.VMEM)
SMEM = pl.BlockSpec(memory_space=pltpu.SMEM)


def dot(a, b):
    return jnp.dot(a, b, preferred_element_type=jnp.float32)


def dot_nt(a, b):
    return lax.dot_general(a, b, (((1,), (1,)), ((), ())), preferred_element_type=jnp.float32)


def sort_q_kernel(rank_q, order_q, *refs):
    q_refs = refs[:2]
    qs, gs, rows, stats = refs[2:]
    n_q = qs.shape[0]
    per_q = QT // HALF
    lines = q_refs[0].shape[0]
    part_q = (q_refs[0].shape[1] - STATS) // HALF

    for a in range(2):
        for n in range(lines):
            for b in range(part_q):
                place = rank_q[(a * lines + n) * part_q + b]
                j = place // per_q
                r = pl.multiple_of(place % per_q * HALF, HALF)
                cut = slice(b * HALF, (b + 1) * HALF)
                for h in range(HEADS):
                    qs[j, pl.ds(h * QT + r, HALF), :] = q_refs[a][n, cut, h * HD:(h + 1) * HD]
                    gs[j, pl.ds(h * QT + r, HALF), :] = q_refs[a][n, cut, (HEADS + h) * HD:(HEADS + h + 1) * HD]
            stats[a * lines + n] = q_refs[a][n, part_q * HALF:, :].astype(jnp.float32)
    quarter = lax.broadcasted_iota(jnp.int32, (STATS, 128), 1) // HALF
    for t in range(n_q * QT // 128):
        line = jnp.zeros((STATS, 128), jnp.float32)
        for u in range(4):
            b = order_q[t * 4 + u]
            column = pl.multiple_of(b % part_q // 2 * 128, 128)
            piece = stats[b // part_q, :, pl.ds(column, 128)]
            piece = pltpu.roll(piece, (u - b % 2 + 4) % 4 * HALF, 1)
            line = jnp.where(quarter == u, piece, line)
        j, c = t // (QT // 128), t % (QT // 128)
        n = 2 * HEADS
        stat = line[:n] + line[n:2 * n] + line[2 * n:3 * n]
        for h in range(HEADS):
            cut = slice(h * QT + c * 128, h * QT + (c + 1) * 128)
            rows[j, 0:1, cut] = stat[h:h + 1] * LOG2E
            rows[j, 1:2, cut] = stat[HEADS + h:HEADS + h + 1]


def sort_q(q_parts, lists_q):
    lines, part, width = q_parts[0].shape
    n_q = 2 * lines * (part - STATS) // QT
    bf, f32 = jnp.bfloat16, jnp.float32
    tiles = jax.ShapeDtypeStruct((n_q, HEADS * QT, HD), bf)
    return pl.pallas_call(
        sort_q_kernel,
        out_shape=(tiles, tiles, jax.ShapeDtypeStruct((n_q, 8, HEADS * QT), f32)),
        in_specs=[SMEM] * 2 + [VMEM] * 2,
        out_specs=(VMEM,) * 3,
        scratch_shapes=[pltpu.VMEM((2 * lines, STATS, width), f32)],
    )(lists_q[0], lists_q[1], *q_parts)


def tile_kernel(rank_q, order_q, sorted_q, rank_k, sorted_k, *refs):
    qs, gs, rows, kv_ref, posq_ref, own_ref, sib_ref, dkv_ref = refs[:8]
    ks, vs, kt, dqt, dqn, dk, dv, todo = refs[8:]
    n_q = qs.shape[0]
    n_k = ks.shape[0]
    per_q = QT // HALF
    per_k = KT // HALF
    half_q = own_ref.shape[0] // HALF
    part_k = kv_ref.shape[0] // HALF

    for b in range(part_k):
        place = rank_k[b]
        i = place // per_k
        r = pl.multiple_of(place % per_k * HALF, HALF)
        cut = slice(b * HALF, (b + 1) * HALF)
        ks[i, pl.ds(r, HALF), :] = kv_ref[cut, :HD]
        vs[i, pl.ds(r, HALF), :] = kv_ref[cut, HD:]

    for i in range(n_k):
        kt[i] = ks[i].astype(jnp.float32).T.astype(jnp.bfloat16)

    dk[...] = jnp.zeros_like(dk)
    dv[...] = jnp.zeros_like(dv)
    dqt[...] = jnp.zeros_like(dqt)

    count = jnp.int32(0)
    dead = jnp.int32(0)
    for j in range(n_q):
        top = sorted_q[j * per_q + per_q - 1]
        for i in range(n_k):
            live = sorted_k[i * per_k] <= top
            todo[count] = jnp.int32(j * n_k + i)
            count = count + live.astype(jnp.int32)
            dead = jnp.where(live, dead, j * n_k + i)
    todo[count] = dead

    within = lax.broadcasted_iota(jnp.int32, (HALF, 128), 0)

    def one(t):
        j = todo[t] // n_k
        i = todo[t] % n_k
        q, g, k, v = qs[j], gs[j], ks[i], vs[i]
        posk = jnp.concatenate([within + sorted_k[i * per_k + b] * HALF for b in range(per_k)], axis=0)
        posk = jnp.concatenate([posk] * (HEADS * QT // 128), axis=1)
        s = dot_nt(k, q)
        p = jnp.where(posk <= posq_ref[j], jnp.exp2(s * (SCALE * LOG2E) - rows[j, 0:1, :]), 0.0)
        dp = dot_nt(v, g)
        ds = (p * (dp - rows[j, 1:2, :])).astype(jnp.bfloat16)
        dv[i] += dot(p.astype(jnp.bfloat16), g)
        dk[i] += dot(ds, q)
        dqt[j] += dot(kt[i], ds)

    def four(t, c):
        for u in range(4):
            one(t * 4 + u)
        return c

    def two(t, c):
        for u in range(2):
            one(t * 2 + u)
        return c

    lax.fori_loop(0, count // 4, four, 0)
    lax.fori_loop(count // 4 * 2, (count + 1) // 2, two, 0)

    for j in range(n_q):
        for h in range(HEADS):
            cut = slice(h * QT, (h + 1) * QT)
            dqn[j, cut, :] = dqt[j, :, cut].T
    for a, out in enumerate((own_ref, sib_ref)):
        for b in range(half_q):
            place = rank_q[a * half_q + b]
            j = place // per_q
            r = pl.multiple_of(place % per_q * HALF, HALF)
            cut = slice(b * HALF, (b + 1) * HALF)
            for h in range(HEADS):
                out[cut, h * HD:(h + 1) * HD] = dqn[j, pl.ds(h * QT + r, HALF), :]
    for b in range(part_k):
        place = rank_k[b]
        i = place // per_k
        r = pl.multiple_of(place % per_k * HALF, HALF)
        cut = slice(b * HALF, (b + 1) * HALF)
        dkv_ref[cut, :HD] = dk[i, pl.ds(r, HALF), :].astype(jnp.bfloat16)
        dkv_ref[cut, HD:] = dv[i, pl.ds(r, HALF), :].astype(jnp.bfloat16)


def tile_grads(q_sorted, kv, lists_q, lists_k):
    rows_q = q_sorted[0].shape[0] * QT
    rows_k = kv.shape[0]
    n_q, n_k = rows_q // QT, rows_k // KT
    rank_q, order_q, sorted_q = lists_q
    rank_k, _, sorted_k = lists_k
    posq = positions(sorted_q).reshape(n_q, 1, QT)
    posq = jnp.concatenate([posq] * HEADS, axis=2)
    bf, f32 = jnp.bfloat16, jnp.float32
    return pl.pallas_call(
        tile_kernel,
        out_shape=(
            jax.ShapeDtypeStruct((rows_q // 2, HEADS * HD), f32),
            jax.ShapeDtypeStruct((rows_q // 2, HEADS * HD), f32),
            jax.ShapeDtypeStruct((rows_k, 2 * HD), bf),
        ),
        in_specs=[SMEM] * 5 + [VMEM] * 5,
        out_specs=(VMEM,) * 3,
        scratch_shapes=[
            pltpu.VMEM((n_k, KT, HD), bf),
            pltpu.VMEM((n_k, KT, HD), bf),
            pltpu.VMEM((n_k, HD, KT), bf),
            pltpu.VMEM((n_q, HD, HEADS * QT), f32),
            pltpu.VMEM((n_q, HEADS * QT, HD), f32),
            pltpu.VMEM((n_k, KT, HD), f32),
            pltpu.VMEM((n_k, KT, HD), f32),
            pltpu.SMEM((n_q * n_k + 1,), jnp.int32),
        ],
        compiler_params=pltpu.CompilerParams(vmem_limit_bytes=40 * 1024 * 1024),
        cost_estimate=pl.CostEstimate(
            flops=rows_q * HEADS * rows_k * HD * 5,
            bytes_accessed=4 * 1024 * 1024,
            transcendentals=rows_q * HEADS * rows_k // 2,
        ),
    )(rank_q, order_q, sorted_q, rank_k, sorted_k, *q_sorted, kv, posq)


def in_order(entries):
    n = entries.shape[0]
    rank = jnp.sum((entries[None, :] < entries[:, None]).astype(jnp.int32), axis=1)
    hit = rank[None, :] == jnp.arange(n, dtype=jnp.int32)[:, None]
    place = jnp.arange(n, dtype=jnp.int32)
    order = jnp.sum(jnp.where(hit, place[None, :], 0), axis=1)
    ordered = jnp.sum(jnp.where(hit, entries[None, :], 0), axis=1)
    return rank, order, ordered


def positions(ordered):
    return (ordered[:, None] * HALF + jnp.arange(HALF, dtype=jnp.int32)[None, :]).reshape(-1)


def pack_q_kernel(q_ref, g_ref, lse_ref, delta_ref, out_ref, wide):
    width = HEADS * HD
    rows = q_ref.shape[0]
    out_ref[:rows, :width] = q_ref[...]
    out_ref[:rows, width:] = g_ref[...]
    out_ref[rows:, :] = jnp.zeros((STATS, 2 * width), jnp.bfloat16)
    wide[...] = jnp.zeros_like(wide)
    n = 2 * HEADS
    for k in range(PIECES):
        wide[k * n:k * n + HEADS, :rows] = lse_ref[...]
        wide[k * n + HEADS:(k + 1) * n, :rows] = delta_ref[...]
    x = wide[...]
    piece = lax.broadcasted_iota(jnp.int32, x.shape, 0) // n
    out = jnp.zeros_like(x)
    for k in range(PIECES):
        part = x.astype(jnp.bfloat16).astype(jnp.float32)
        x = x - part
        out = jnp.where(piece == k, part, out)
    out_ref[rows:, :128] = out.astype(jnp.bfloat16)


def pack_q(queries, out_grad, log_sum, delta):
    rows = queries.shape[0]
    return pl.pallas_call(
        pack_q_kernel,
        out_shape=jax.ShapeDtypeStruct((rows + STATS, 2 * HEADS * HD), jnp.bfloat16),
        in_specs=[VMEM] * 4,
        out_specs=VMEM,
        scratch_shapes=[pltpu.VMEM((STATS, 128), jnp.float32)],
    )(queries, out_grad, log_sum.T, delta.T)


def join(parts):
    rows = parts[0].shape[0] - STATS
    stats = jnp.concatenate([p[rows:, :128] for p in parts], axis=1)
    return jnp.concatenate([p[:rows] for p in parts] + [stats], axis=0)


def from_offset(x, stage, d):
    pairs = []
    for ix in range(4):
        for iy in range(4):
            for core in range(2):
                tx, ty = ((ix + d) % 4, iy) if core == stage else (ix, (iy + d) % 4)
                pairs.append((place(ix, iy, core), place(tx, ty, core)))
    return lax.ppermute(x, ("x", "yl", "yh", "core"), pairs)


def place(ix, iy, core):
    return ((ix * 2 + iy % 2) * 2 + iy // 2) * 2 + core


def other_core(x):
    return lax.ppermute(x, "core", [(0, 1), (1, 0)])


def look_up(table, index):
    spot = jnp.arange(table.shape[0], dtype=jnp.int32)
    return jnp.sum(jnp.where(index[:, None] == spot[None, :], table[None, :], 0), axis=1)


def both_blocks(device):
    return (2 * device[:, None] + jnp.arange(2, dtype=jnp.int32)[None, :]).reshape(-1)


def local(queries, keys, values, out_grad, log_sum, delta, block_table):
    rows = queries.shape[0]
    width = HEADS * HD
    nx, nyl, nz, nyh, nc = (lax.axis_size(a) for a in ("x", "yl", "z", "yh", "core"))
    ix, iyl, iz, iyh, ic = (lax.axis_index(a) for a in ("x", "yl", "z", "yh", "core"))
    iy = iyh * nyl + iyl

    kv = jnp.concatenate([jnp.broadcast_to(x[None], (nz,) + x.shape) for x in (keys, values)], axis=2)
    kv = lax.all_to_all(kv, "z", split_axis=0, concat_axis=0, tiled=True)
    kv = kv.reshape(nz * rows, 2 * HD)
    packed = pack_q(queries, out_grad, log_sum, delta)
    line = join([packed] + [from_offset(packed, 0, d) for d in (1, 2, 3)])
    q_own = jnp.stack([line] + [from_offset(line, 1, d) for d in (1, 2, 3)])
    table, q_own = lax.optimization_barrier((block_table, q_own))
    q_sib = other_core(q_own)

    spot = jnp.arange(nz, dtype=jnp.int32)
    lists_k = in_order(look_up(table, both_blocks(((spot * nyh + iyh) * nc + ic) * nx * nyl + ix * nyl + iyl)))
    at = []
    for c in (ic, nc - 1 - ic):
        along_x, along_y = jnp.where(c == 0, spot % 4, spot // 4), jnp.where(c == 0, spot // 4, spot % 4)
        x, y = (ix - along_x) % nx, (iy - along_y) % (nyl * nyh)
        at.append(((x * nyl + y % nyl) * nz + iz) * nyh * nc + y // nyl * nc + c)
    lists_q = in_order(look_up(table, both_blocks(jnp.concatenate(at))))

    dq, dq_sib, dkv = tile_grads(sort_q([q_own, q_sib], lists_q), kv, lists_q, lists_k)

    dkv = lax.all_to_all(dkv.reshape(nz, rows, 2 * HD), "z", split_axis=0, concat_axis=0, tiled=True)
    dq = dq + other_core(dq_sib)
    near, far = dq[:4 * rows], dq.astype(jnp.bfloat16)
    far = far.reshape(4, 4 * rows, width)
    for d in (1, 2, 3):
        near = near + from_offset(far[d], 1, 4 - d).astype(jnp.float32)
    near = near.reshape(4, rows, width)
    total = near[0]
    for d in (1, 2, 3):
        total = total + from_offset(near[d], 0, 4 - d)
    q_grad = (total * SCALE).astype(jnp.bfloat16)
    dkv = jnp.sum(dkv.astype(jnp.float32), axis=0)
    k_grad = (dkv[:, :HD] * SCALE).astype(jnp.bfloat16)
    v_grad = dkv[:, HD:].astype(jnp.bfloat16)
    return (q_grad, k_grad, v_grad)


def solution(mesh):
    fine = Mesh(mesh.devices.reshape(4, 2, 16, 2, 2), ("x", "yl", "z", "yh", "core"))
    q_rows = P(("x", "yl", "z", "yh", "core"), None)
    k_rows = P(("z", "yh", "core", "x", "yl"), None)
    return jax.shard_map(
        local,
        mesh=fine,
        in_specs=(q_rows, k_rows, k_rows, q_rows, q_rows, q_rows, P()),
        out_specs=(q_rows, k_rows, k_rows),
        check_vma=False,
    )
```

```python
import jax
import jax.numpy as jnp
from jax import lax
from jax.experimental import pallas as pl
from jax.experimental.pallas import tpu as pltpu
from jax.sharding import Mesh, PartitionSpec as P

HEADS = 2
HD = 128
HALF = 32
SCALE = HD ** (-0.5)
LOG2E = 1.4426950408889634
PIECES = 3
STATS = 16
QT = 256
KT = 256
VMEM = pl.BlockSpec(memory_space=pltpu.VMEM)
SMEM = pl.BlockSpec(memory_space=pltpu.SMEM)


def dot(a, b):
    return jnp.dot(a, b, preferred_element_type=jnp.float32)


def dot_nt(a, b):
    return lax.dot_general(a, b, (((1,), (1,)), ((), ())), preferred_element_type=jnp.float32)


def tile_kernel(rank_q, order_q, sorted_q, rank_k, sorted_k, *refs):
    q_refs = refs[:2]
    kv_ref, posq_ref, own_ref, sib_ref, dkv_ref = refs[2:7]
    qs, gs, stats, rows, ks, vs, kt, dqt, dqn, dk, dv, todo = refs[7:]
    n_q = qs.shape[0]
    n_k = ks.shape[0]
    per_q = QT // HALF
    per_k = KT // HALF
    lines = q_refs[0].shape[0]
    part_q = (q_refs[0].shape[1] - STATS) // HALF
    part_k = kv_ref.shape[0] // HALF

    for a in range(2):
        for n in range(lines):
            for b in range(part_q):
                place = rank_q[(a * lines + n) * part_q + b]
                j = place // per_q
                r = pl.multiple_of(place % per_q * HALF, HALF)
                cut = slice(b * HALF, (b + 1) * HALF)
                for h in range(HEADS):
                    qs[j, pl.ds(h * QT + r, HALF), :] = q_refs[a][n, cut, h * HD:(h + 1) * HD]
                    gs[j, pl.ds(h * QT + r, HALF), :] = q_refs[a][n, cut, (HEADS + h) * HD:(HEADS + h + 1) * HD]
            stats[a * lines + n] = q_refs[a][n, part_q * HALF:, :].astype(jnp.float32)
    for b in range(part_k):
        place = rank_k[b]
        i = place // per_k
        r = pl.multiple_of(place % per_k * HALF, HALF)
        cut = slice(b * HALF, (b + 1) * HALF)
        ks[i, pl.ds(r, HALF), :] = kv_ref[cut, :HD]
        vs[i, pl.ds(r, HALF), :] = kv_ref[cut, HD:]

    quarter = lax.broadcasted_iota(jnp.int32, (STATS, 128), 1) // HALF
    for t in range(n_q * QT // 128):
        line = jnp.zeros((STATS, 128), jnp.float32)
        for u in range(4):
            b = order_q[t * 4 + u]
            column = pl.multiple_of(b % part_q // 2 * 128, 128)
            piece = stats[b // part_q, :, pl.ds(column, 128)]
            piece = pltpu.roll(piece, (u - b % 2 + 4) % 4 * HALF, 1)
            line = jnp.where(quarter == u, piece, line)
        j, c = t // (QT // 128), t % (QT // 128)
        n = 2 * HEADS
        stat = line[:n] + line[n:2 * n] + line[2 * n:3 * n]
        for h in range(HEADS):
            cut = slice(h * QT + c * 128, h * QT + (c + 1) * 128)
            rows[j, 0:1, cut] = stat[h:h + 1] * LOG2E
            rows[j, 1:2, cut] = stat[HEADS + h:HEADS + h + 1]

    for i in range(n_k):
        kt[i] = ks[i].astype(jnp.float32).T.astype(jnp.bfloat16)

    dk[...] = jnp.zeros_like(dk)
    dv[...] = jnp.zeros_like(dv)
    dqt[...] = jnp.zeros_like(dqt)

    count = jnp.int32(0)
    dead = jnp.int32(0)
    for j in range(n_q):
        top = sorted_q[j * per_q + per_q - 1]
        for i in range(n_k):
            live = sorted_k[i * per_k] <= top
            todo[count] = jnp.int32(j * n_k + i)
            count = count + live.astype(jnp.int32)
            dead = jnp.where(live, dead, j * n_k + i)
    todo[count] = dead

    within = lax.broadcasted_iota(jnp.int32, (HALF, 128), 0)

    def one(t):
        j = todo[t] // n_k
        i = todo[t] % n_k
        q, g, k, v = qs[j], gs[j], ks[i], vs[i]
        posk = jnp.concatenate([within + sorted_k[i * per_k + b] * HALF for b in range(per_k)], axis=0)
        posk = jnp.concatenate([posk] * (HEADS * QT // 128), axis=1)
        s = dot_nt(k, q)
        p = jnp.where(posk <= posq_ref[j], jnp.exp2(s * (SCALE * LOG2E) - rows[j, 0:1, :]), 0.0)
        dp = dot_nt(v, g)
        ds = (p * (dp - rows[j, 1:2, :])).astype(jnp.bfloat16)
        dv[i] += dot(p.astype(jnp.bfloat16), g)
        dk[i] += dot(ds, q)
        dqt[j] += dot(kt[i], ds)

    def four(t, c):
        for u in range(4):
            one(t * 4 + u)
        return c

    def two(t, c):
        for u in range(2):
            one(t * 2 + u)
        return c

    lax.fori_loop(0, count // 4, four, 0)
    lax.fori_loop(count // 4 * 2, (count + 1) // 2, two, 0)

    for j in range(n_q):
        for h in range(HEADS):
            cut = slice(h * QT, (h + 1) * QT)
            dqn[j, cut, :] = dqt[j, :, cut].T
    for a, out in enumerate((own_ref, sib_ref)):
        for b in range(lines * part_q):
            place = rank_q[a * lines * part_q + b]
            j = place // per_q
            r = pl.multiple_of(place % per_q * HALF, HALF)
            cut = slice(b * HALF, (b + 1) * HALF)
            for h in range(HEADS):
                out[cut, h * HD:(h + 1) * HD] = dqn[j, pl.ds(h * QT + r, HALF), :].astype(out.dtype)
    for b in range(part_k):
        place = rank_k[b]
        i = place // per_k
        r = pl.multiple_of(place % per_k * HALF, HALF)
        cut = slice(b * HALF, (b + 1) * HALF)
        dkv_ref[cut, :HD] = dk[i, pl.ds(r, HALF), :].astype(jnp.bfloat16)
        dkv_ref[cut, HD:] = dv[i, pl.ds(r, HALF), :].astype(jnp.bfloat16)


def tile_grads(q_parts, kv, lists_q, lists_k):
    lines, part = q_parts[0].shape[:2]
    rows_q = 2 * lines * (part - STATS)
    rows_k = kv.shape[0]
    n_q, n_k = rows_q // QT, rows_k // KT
    rank_q, order_q, sorted_q = lists_q
    rank_k, _, sorted_k = lists_k
    posq = positions(sorted_q).reshape(n_q, 1, QT)
    posq = jnp.concatenate([posq] * HEADS, axis=2)
    bf, f32 = jnp.bfloat16, jnp.float32
    return pl.pallas_call(
        tile_kernel,
        out_shape=(
            jax.ShapeDtypeStruct((rows_q // 2, HEADS * HD), f32),
            jax.ShapeDtypeStruct((rows_q // 2, HEADS * HD), bf),
            jax.ShapeDtypeStruct((rows_k, 2 * HD), bf),
        ),
        in_specs=[SMEM] * 5 + [VMEM] * 4,
        out_specs=(VMEM,) * 3,
        scratch_shapes=[
            pltpu.VMEM((n_q, HEADS * QT, HD), bf),
            pltpu.VMEM((n_q, HEADS * QT, HD), bf),
            pltpu.VMEM((2 * lines, STATS, 512), f32),
            pltpu.VMEM((n_q, 8, HEADS * QT), f32),
            pltpu.VMEM((n_k, KT, HD), bf),
            pltpu.VMEM((n_k, KT, HD), bf),
            pltpu.VMEM((n_k, HD, KT), bf),
            pltpu.VMEM((n_q, HD, HEADS * QT), f32),
            pltpu.VMEM((n_q, HEADS * QT, HD), f32),
            pltpu.VMEM((n_k, KT, HD), f32),
            pltpu.VMEM((n_k, KT, HD), f32),
            pltpu.SMEM((n_q * n_k + 1,), jnp.int32),
        ],
        compiler_params=pltpu.CompilerParams(vmem_limit_bytes=40 * 1024 * 1024),
        cost_estimate=pl.CostEstimate(
            flops=rows_q * HEADS * rows_k * HD * 5,
            bytes_accessed=4 * 1024 * 1024,
            transcendentals=rows_q * HEADS * rows_k // 2,
        ),
    )(rank_q, order_q, sorted_q, rank_k, sorted_k, *q_parts, kv, posq)


def in_order(entries):
    n = entries.shape[0]
    rank = jnp.sum((entries[None, :] < entries[:, None]).astype(jnp.int32), axis=1)
    hit = rank[None, :] == jnp.arange(n, dtype=jnp.int32)[:, None]
    place = jnp.arange(n, dtype=jnp.int32)
    order = jnp.sum(jnp.where(hit, place[None, :], 0), axis=1)
    ordered = jnp.sum(jnp.where(hit, entries[None, :], 0), axis=1)
    return rank, order, ordered


def positions(ordered):
    return (ordered[:, None] * HALF + jnp.arange(HALF, dtype=jnp.int32)[None, :]).reshape(-1)


def pack_q_kernel(q_ref, g_ref, lse_ref, delta_ref, out_ref, wide):
    width = HEADS * HD
    rows = q_ref.shape[0]
    out_ref[:rows, :width] = q_ref[...]
    out_ref[:rows, width:] = g_ref[...]
    out_ref[rows:, :] = jnp.zeros((STATS, 2 * width), jnp.bfloat16)
    wide[...] = jnp.zeros_like(wide)
    n = 2 * HEADS
    for k in range(PIECES):
        wide[k * n:k * n + HEADS, :rows] = lse_ref[...]
        wide[k * n + HEADS:(k + 1) * n, :rows] = delta_ref[...]
    x = wide[...]
    piece = lax.broadcasted_iota(jnp.int32, x.shape, 0) // n
    out = jnp.zeros_like(x)
    for k in range(PIECES):
        part = x.astype(jnp.bfloat16).astype(jnp.float32)
        x = x - part
        out = jnp.where(piece == k, part, out)
    out_ref[rows:, :128] = out.astype(jnp.bfloat16)


def pack_q(queries, out_grad, log_sum, delta):
    rows = queries.shape[0]
    return pl.pallas_call(
        pack_q_kernel,
        out_shape=jax.ShapeDtypeStruct((rows + STATS, 2 * HEADS * HD), jnp.bfloat16),
        in_specs=[VMEM] * 4,
        out_specs=VMEM,
        scratch_shapes=[pltpu.VMEM((STATS, 128), jnp.float32)],
    )(queries, out_grad, log_sum.T, delta.T)


def join(parts):
    rows = parts[0].shape[0] - STATS
    stats = jnp.concatenate([p[rows:, :128] for p in parts], axis=1)
    return jnp.concatenate([p[:rows] for p in parts] + [stats], axis=0)


def from_offset(x, stage, d):
    pairs = []
    for ix in range(4):
        for iy in range(4):
            for core in range(2):
                tx, ty = ((ix + d) % 4, iy) if core == stage else (ix, (iy + d) % 4)
                pairs.append((place(ix, iy, core), place(tx, ty, core)))
    return lax.ppermute(x, ("x", "yl", "yh", "core"), pairs)


def place(ix, iy, core):
    return ((ix * 2 + iy % 2) * 2 + iy // 2) * 2 + core


def other_core(x):
    return lax.ppermute(x, "core", [(0, 1), (1, 0)])


def look_up(table, index):
    spot = jnp.arange(table.shape[0], dtype=jnp.int32)
    return jnp.sum(jnp.where(index[:, None] == spot[None, :], table[None, :], 0), axis=1)


def both_blocks(device):
    return (2 * device[:, None] + jnp.arange(2, dtype=jnp.int32)[None, :]).reshape(-1)


def local(queries, keys, values, out_grad, log_sum, delta, block_table):
    rows = queries.shape[0]
    width = HEADS * HD
    nx, nyl, nz, nyh, nc = (lax.axis_size(a) for a in ("x", "yl", "z", "yh", "core"))
    ix, iyl, iz, iyh, ic = (lax.axis_index(a) for a in ("x", "yl", "z", "yh", "core"))
    iy = iyh * nyl + iyl

    kv = jnp.concatenate([keys, values], axis=1)
    kv = lax.all_to_all(jnp.broadcast_to(kv[None], (nz,) + kv.shape), "z", split_axis=0, concat_axis=0, tiled=True)
    kv = kv.reshape(nz * rows, 2 * HD)
    packed = pack_q(queries, out_grad, log_sum, delta)
    line = join([packed] + [from_offset(packed, 0, d) for d in (1, 2, 3)])
    q_own = jnp.stack([line] + [from_offset(line, 1, d) for d in (1, 2, 3)])
    table, q_own = lax.optimization_barrier((block_table, q_own))
    q_sib = other_core(q_own)

    spot = jnp.arange(nz, dtype=jnp.int32)
    lists_k = in_order(look_up(table, both_blocks(((spot * nyh + iyh) * nc + ic) * nx * nyl + ix * nyl + iyl)))
    at = []
    for c in (ic, nc - 1 - ic):
        along_x, along_y = jnp.where(c == 0, spot % 4, spot // 4), jnp.where(c == 0, spot // 4, spot % 4)
        x, y = (ix - along_x) % nx, (iy - along_y) % (nyl * nyh)
        at.append(((x * nyl + y % nyl) * nz + iz) * nyh * nc + y // nyl * nc + c)
    lists_q = in_order(look_up(table, both_blocks(jnp.concatenate(at))))

    dq, dq_sib, dkv = tile_grads([q_own, q_sib], kv, lists_q, lists_k)

    dkv = lax.all_to_all(dkv.reshape(nz, rows, 2 * HD), "z", split_axis=0, concat_axis=0, tiled=True)
    dq = dq + other_core(dq_sib).astype(jnp.float32)
    near, far = dq[:4 * rows], dq.astype(jnp.bfloat16)
    far = far.reshape(4, 4 * rows, width)
    for d in (1, 2, 3):
        near = near + from_offset(far[d], 1, 4 - d).astype(jnp.float32)
    near = near.reshape(4, rows, width)
    total = near[0]
    for d in (1, 2, 3):
        total = total + from_offset(near[d], 0, 4 - d)
    q_grad = (total * SCALE).astype(jnp.bfloat16)
    dkv = jnp.sum(dkv.astype(jnp.float32), axis=0)
    k_grad = (dkv[:, :HD] * SCALE).astype(jnp.bfloat16)
    v_grad = dkv[:, HD:].astype(jnp.bfloat16)
    return (q_grad, k_grad, v_grad)


def solution(mesh):
    fine = Mesh(mesh.devices.reshape(4, 2, 16, 2, 2), ("x", "yl", "z", "yh", "core"))
    q_rows = P(("x", "yl", "z", "yh", "core"), None)
    k_rows = P(("z", "yh", "core", "x", "yl"), None)
    return jax.shard_map(
        local,
        mesh=fine,
        in_specs=(q_rows, k_rows, k_rows, q_rows, q_rows, q_rows, P()),
        out_specs=(q_rows, k_rows, k_rows),
        check_vma=False,
    )
```

```python
import jax
import jax.numpy as jnp
from jax import lax
from jax.experimental import pallas as pl
from jax.experimental.pallas import tpu as pltpu
from jax.sharding import Mesh, PartitionSpec as P

HEADS = 2
HD = 128
HALF = 32
SCALE = HD ** (-0.5)
LOG2E = 1.4426950408889634
PIECES = 3
STATS = 16
QT = 256
KT = 256
VMEM = pl.BlockSpec(memory_space=pltpu.VMEM)
SMEM = pl.BlockSpec(memory_space=pltpu.SMEM)


def dot(a, b):
    return jnp.dot(a, b, preferred_element_type=jnp.float32)


def dot_nt(a, b):
    return lax.dot_general(a, b, (((1,), (1,)), ((), ())), preferred_element_type=jnp.float32)


def tile_kernel(rank_q, order_q, sorted_q, rank_k, sorted_k, *refs):
    q_refs = refs[:2]
    kv_ref, posq_ref, own_ref, sib_ref, dkv_ref = refs[2:7]
    qs, gs, stats, rows, ks, vs, kt, dqt, dqn, dk, dv, todo = refs[7:]
    n_q = qs.shape[0]
    n_k = ks.shape[0]
    per_q = QT // HALF
    per_k = KT // HALF
    lines = q_refs[0].shape[0]
    part_q = (q_refs[0].shape[1] - STATS) // HALF
    part_k = kv_ref.shape[0] // HALF

    for a in range(2):
        for n in range(lines):
            for b in range(part_q):
                place = rank_q[(a * lines + n) * part_q + b]
                j = place // per_q
                r = pl.multiple_of(place % per_q * HALF, HALF)
                cut = slice(b * HALF, (b + 1) * HALF)
                for h in range(HEADS):
                    qs[j, pl.ds(h * QT + r, HALF), :] = q_refs[a][n, cut, h * HD:(h + 1) * HD]
                    gs[j, pl.ds(h * QT + r, HALF), :] = q_refs[a][n, cut, (HEADS + h) * HD:(HEADS + h + 1) * HD]
            stats[a * lines + n] = q_refs[a][n, part_q * HALF:, :].astype(jnp.float32)
    for b in range(part_k):
        place = rank_k[b]
        i = place // per_k
        r = pl.multiple_of(place % per_k * HALF, HALF)
        cut = slice(b * HALF, (b + 1) * HALF)
        ks[i, pl.ds(r, HALF), :] = kv_ref[cut, :HD]
        vs[i, pl.ds(r, HALF), :] = kv_ref[cut, HD:]

    quarter = lax.broadcasted_iota(jnp.int32, (STATS, 128), 1) // HALF
    for t in range(n_q * QT // 128):
        line = jnp.zeros((STATS, 128), jnp.float32)
        for u in range(4):
            b = order_q[t * 4 + u]
            column = pl.multiple_of(b % part_q // 2 * 128, 128)
            piece = stats[b // part_q, :, pl.ds(column, 128)]
            piece = pltpu.roll(piece, (u - b % 2 + 4) % 4 * HALF, 1)
            line = jnp.where(quarter == u, piece, line)
        j, c = t // (QT // 128), t % (QT // 128)
        n = 2 * HEADS
        stat = line[:n] + line[n:2 * n] + line[2 * n:3 * n]
        for h in range(HEADS):
            cut = slice(h * QT + c * 128, h * QT + (c + 1) * 128)
            rows[j, 0:1, cut] = stat[h:h + 1] * LOG2E
            rows[j, 1:2, cut] = stat[HEADS + h:HEADS + h + 1]

    for i in range(n_k):
        kt[i] = ks[i].astype(jnp.float32).T.astype(jnp.bfloat16)

    dk[...] = jnp.zeros_like(dk)
    dv[...] = jnp.zeros_like(dv)
    dqt[...] = jnp.zeros_like(dqt)

    count = jnp.int32(0)
    dead = jnp.int32(0)
    for j in range(n_q):
        top = sorted_q[j * per_q + per_q - 1]
        for i in range(n_k):
            live = sorted_k[i * per_k] <= top
            todo[count] = jnp.int32(j * n_k + i)
            count = count + live.astype(jnp.int32)
            dead = jnp.where(live, dead, j * n_k + i)
    todo[count] = dead

    within = lax.broadcasted_iota(jnp.int32, (HALF, 128), 0)

    def one(t):
        j = todo[t] // n_k
        i = todo[t] % n_k
        q, g, k, v = qs[j], gs[j], ks[i], vs[i]
        posk = jnp.concatenate([within + sorted_k[i * per_k + b] * HALF for b in range(per_k)], axis=0)
        posk = jnp.concatenate([posk] * (HEADS * QT // 128), axis=1)
        s = dot_nt(k, q)
        p = jnp.where(posk <= posq_ref[j], jnp.exp2(s * (SCALE * LOG2E) - rows[j, 0:1, :]), 0.0)
        dp = dot_nt(v, g)
        ds = (p * (dp - rows[j, 1:2, :])).astype(jnp.bfloat16)
        dv[i] += dot(p.astype(jnp.bfloat16), g)
        dk[i] += dot(ds, q)
        dqt[j] += dot(kt[i], ds)

    def four(t, c):
        for u in range(4):
            one(t * 4 + u)
        return c

    def two(t, c):
        for u in range(2):
            one(t * 2 + u)
        return c

    lax.fori_loop(0, count // 4, four, 0)
    lax.fori_loop(count // 4 * 2, (count + 1) // 2, two, 0)

    for j in range(n_q):
        for h in range(HEADS):
            cut = slice(h * QT, (h + 1) * QT)
            dqn[j, cut, :] = dqt[j, :, cut].T
    for a, out in enumerate((own_ref, sib_ref)):
        for b in range(lines * part_q):
            place = rank_q[a * lines * part_q + b]
            j = place // per_q
            r = pl.multiple_of(place % per_q * HALF, HALF)
            cut = slice(b * HALF, (b + 1) * HALF)
            for h in range(HEADS):
                out[cut, h * HD:(h + 1) * HD] = dqn[j, pl.ds(h * QT + r, HALF), :].astype(out.dtype)
    for b in range(part_k):
        place = rank_k[b]
        i = place // per_k
        r = pl.multiple_of(place % per_k * HALF, HALF)
        cut = slice(b * HALF, (b + 1) * HALF)
        dkv_ref[cut, :HD] = dk[i, pl.ds(r, HALF), :].astype(jnp.bfloat16)
        dkv_ref[cut, HD:] = dv[i, pl.ds(r, HALF), :].astype(jnp.bfloat16)


def tile_grads(q_parts, kv, lists_q, lists_k):
    lines, part = q_parts[0].shape[:2]
    rows_q = 2 * lines * (part - STATS)
    rows_k = kv.shape[0]
    n_q, n_k = rows_q // QT, rows_k // KT
    rank_q, order_q, sorted_q = lists_q
    rank_k, _, sorted_k = lists_k
    posq = positions(sorted_q).reshape(n_q, 1, QT)
    posq = jnp.concatenate([posq] * HEADS, axis=2)
    bf, f32 = jnp.bfloat16, jnp.float32
    return pl.pallas_call(
        tile_kernel,
        out_shape=(
            jax.ShapeDtypeStruct((rows_q // 2, HEADS * HD), f32),
            jax.ShapeDtypeStruct((rows_q // 2, HEADS * HD), bf),
            jax.ShapeDtypeStruct((rows_k, 2 * HD), bf),
        ),
        in_specs=[SMEM] * 5 + [VMEM] * 4,
        out_specs=(VMEM,) * 3,
        scratch_shapes=[
            pltpu.VMEM((n_q, HEADS * QT, HD), bf),
            pltpu.VMEM((n_q, HEADS * QT, HD), bf),
            pltpu.VMEM((2 * lines, STATS, 512), f32),
            pltpu.VMEM((n_q, 8, HEADS * QT), f32),
            pltpu.VMEM((n_k, KT, HD), bf),
            pltpu.VMEM((n_k, KT, HD), bf),
            pltpu.VMEM((n_k, HD, KT), bf),
            pltpu.VMEM((n_q, HD, HEADS * QT), f32),
            pltpu.VMEM((n_q, HEADS * QT, HD), f32),
            pltpu.VMEM((n_k, KT, HD), f32),
            pltpu.VMEM((n_k, KT, HD), f32),
            pltpu.SMEM((n_q * n_k + 1,), jnp.int32),
        ],
        compiler_params=pltpu.CompilerParams(vmem_limit_bytes=40 * 1024 * 1024),
        cost_estimate=pl.CostEstimate(
            flops=rows_q * HEADS * rows_k * HD * 5,
            bytes_accessed=4 * 1024 * 1024,
            transcendentals=rows_q * HEADS * rows_k // 2,
        ),
    )(rank_q, order_q, sorted_q, rank_k, sorted_k, *q_parts, kv, posq)


def in_order(entries):
    n = entries.shape[0]
    rank = jnp.sum((entries[None, :] < entries[:, None]).astype(jnp.int32), axis=1)
    hit = rank[None, :] == jnp.arange(n, dtype=jnp.int32)[:, None]
    place = jnp.arange(n, dtype=jnp.int32)
    order = jnp.sum(jnp.where(hit, place[None, :], 0), axis=1)
    ordered = jnp.sum(jnp.where(hit, entries[None, :], 0), axis=1)
    return rank, order, ordered


def positions(ordered):
    return (ordered[:, None] * HALF + jnp.arange(HALF, dtype=jnp.int32)[None, :]).reshape(-1)


def pack_q_kernel(q_ref, g_ref, lse_ref, delta_ref, out_ref, wide):
    width = HEADS * HD
    rows = q_ref.shape[0]
    out_ref[:rows, :width] = q_ref[...]
    out_ref[:rows, width:] = g_ref[...]
    out_ref[rows:, :] = jnp.zeros((STATS, 2 * width), jnp.bfloat16)
    wide[...] = jnp.zeros_like(wide)
    n = 2 * HEADS
    for k in range(PIECES):
        wide[k * n:k * n + HEADS, :rows] = lse_ref[...]
        wide[k * n + HEADS:(k + 1) * n, :rows] = delta_ref[...]
    x = wide[...]
    piece = lax.broadcasted_iota(jnp.int32, x.shape, 0) // n
    out = jnp.zeros_like(x)
    for k in range(PIECES):
        part = x.astype(jnp.bfloat16).astype(jnp.float32)
        x = x - part
        out = jnp.where(piece == k, part, out)
    out_ref[rows:, :128] = out.astype(jnp.bfloat16)


def pack_q(queries, out_grad, log_sum, delta):
    rows = queries.shape[0]
    return pl.pallas_call(
        pack_q_kernel,
        out_shape=jax.ShapeDtypeStruct((rows + STATS, 2 * HEADS * HD), jnp.bfloat16),
        in_specs=[VMEM] * 4,
        out_specs=VMEM,
        scratch_shapes=[pltpu.VMEM((STATS, 128), jnp.float32)],
    )(queries, out_grad, log_sum.T, delta.T)


def join(parts):
    rows = parts[0].shape[0] - STATS
    stats = jnp.concatenate([p[rows:, :128] for p in parts], axis=1)
    return jnp.concatenate([p[:rows] for p in parts] + [stats], axis=0)


def from_offset(x, stage, d):
    pairs = []
    for ix in range(4):
        for iy in range(4):
            for core in range(2):
                tx, ty = ((ix + d) % 4, iy) if core == stage else (ix, (iy + d) % 4)
                pairs.append((place(ix, iy, core), place(tx, ty, core)))
    return lax.ppermute(x, ("x", "yl", "yh", "core"), pairs)


def place(ix, iy, core):
    return ((ix * 2 + iy % 2) * 2 + iy // 2) * 2 + core


def other_core(x):
    return lax.ppermute(x, "core", [(0, 1), (1, 0)])


def look_up(table, index):
    spot = jnp.arange(table.shape[0], dtype=jnp.int32)
    return jnp.sum(jnp.where(index[:, None] == spot[None, :], table[None, :], 0), axis=1)


def both_blocks(device):
    return (2 * device[:, None] + jnp.arange(2, dtype=jnp.int32)[None, :]).reshape(-1)


def local(queries, keys, values, out_grad, log_sum, delta, block_table):
    rows = queries.shape[0]
    width = HEADS * HD
    nx, nyl, nz, nyh, nc = (lax.axis_size(a) for a in ("x", "yl", "z", "yh", "core"))
    ix, iyl, iz, iyh, ic = (lax.axis_index(a) for a in ("x", "yl", "z", "yh", "core"))
    iy = iyh * nyl + iyl

    kv = jnp.concatenate([keys, values], axis=1)
    kv = lax.all_to_all(jnp.broadcast_to(kv[None], (nz,) + kv.shape), "z", split_axis=0, concat_axis=0, tiled=True)
    kv = kv.reshape(nz * rows, 2 * HD)
    packed = pack_q(queries, out_grad, log_sum, delta)
    line = join([packed] + [from_offset(packed, 0, d) for d in (1, 2, 3)])
    q_own = jnp.stack([line] + [from_offset(line, 1, d) for d in (1, 2, 3)])
    table, q_own = lax.optimization_barrier((block_table, q_own))
    q_sib = other_core(q_own)

    spot = jnp.arange(nz, dtype=jnp.int32)
    lists_k = in_order(look_up(table, both_blocks(((spot * nyh + iyh) * nc + ic) * nx * nyl + ix * nyl + iyl)))
    at = []
    for c in (ic, nc - 1 - ic):
        along_x, along_y = jnp.where(c == 0, spot % 4, spot // 4), jnp.where(c == 0, spot // 4, spot % 4)
        x, y = (ix - along_x) % nx, (iy - along_y) % (nyl * nyh)
        at.append(((x * nyl + y % nyl) * nz + iz) * nyh * nc + y // nyl * nc + c)
    lists_q = in_order(look_up(table, both_blocks(jnp.concatenate(at))))

    dq, dq_sib, dkv = tile_grads([q_own, q_sib], kv, lists_q, lists_k)

    dkv = lax.all_to_all(dkv.reshape(nz, rows, 2 * HD), "z", split_axis=0, concat_axis=0, tiled=True)
    dq = dq + other_core(dq_sib).astype(jnp.float32)
    near, far = dq[:4 * rows], dq.astype(jnp.bfloat16)
    far = far.reshape(4, 4 * rows, width)
    for d in (1, 2, 3):
        near = near + from_offset(far[d], 1, 4 - d).astype(jnp.float32)
    near = near.reshape(4, rows, width)
    total = near[0]
    for d in (1, 2, 3):
        total = total + from_offset(near[d].astype(jnp.bfloat16), 0, 4 - d).astype(jnp.float32)
    q_grad = (total * SCALE).astype(jnp.bfloat16)
    dkv = jnp.sum(dkv.astype(jnp.float32), axis=0)
    k_grad = (dkv[:, :HD] * SCALE).astype(jnp.bfloat16)
    v_grad = dkv[:, HD:].astype(jnp.bfloat16)
    return (q_grad, k_grad, v_grad)


def solution(mesh):
    fine = Mesh(mesh.devices.reshape(4, 2, 16, 2, 2), ("x", "yl", "z", "yh", "core"))
    q_rows = P(("x", "yl", "z", "yh", "core"), None)
    k_rows = P(("z", "yh", "core", "x", "yl"), None)
    return jax.shard_map(
        local,
        mesh=fine,
        in_specs=(q_rows, k_rows, k_rows, q_rows, q_rows, q_rows, P()),
        out_specs=(q_rows, k_rows, k_rows),
        check_vma=False,
    )
```
